1024 devices in a mesh: dp: 32 (over z, core), owner: 32 (over y, x).
Axes of the slice: x: 4, y: 8, z: 16, core: 2. Of those that a mesh axis runs over, the one named last changes fastest.
Arguments:
- acts: bfloat16 [32768, 4096], P('dp'), may hold values from -33 to 33
- dout: bfloat16 [32768, 8, 512], P('dp', None, 'owner'), may hold values from -2 to 2
- left_stats: float32 [128, 512, 512], P('owner', 'dp'), may hold values from -3 to 3
- right_stats: float32 [128, 512, 512], P('owner', 'dp'), may hold values from -3 to 3
- left_root: bfloat16 [128, 512, 512], P('owner', 'dp'), may hold values from -10 to 10
- right_root: bfloat16 [128, 512, 512], P('owner'), may hold values from -10 to 10
- owner_of: int32 [64, 1], replicated, may hold values from 0 to 31; in each aligned block of 64 rows (0 to 63, 64 to 127, ...) at most 4 rows name the same one
- counters: int32 [64], replicated, may hold values from 0 to 49
Outputs:
- left_out: float32 [128, 512, 512], P('owner', 'dp')
- right_out: float32 [128, 512, 512], P('owner', 'dp')
- update: bfloat16 [8, 512, 8, 512], P(None, 'dp', None, 'owner')
The draws below stay inside these ranges and needn't reach their ends.
Inputs may be any that keep to these rules, and one draw needn't show every extreme that they name: `owner_of`: every owner owns at least one block and at most 4; some owner owns exactly 4.
All inputs are finite; a program needn't handle non-finite values.
Results may differ from the reference program's by a relative error of at most 0.009.
Values may be sent and summed in bfloat16 or wider, within the bound.
A program may use at most 64 MiB of HBM per device.

```python
import math
import jax
import jax.numpy as jnp
import numpy as np
from jax import lax

B = 512
FEATS = 4096
D = 4096
WARMUP = 25
BR = 8
BC = 8
NB = 64
SLOTS = 4
TOKENS = 32768
N_OWNER = 32


def draw_acts(key, part):
    key = jax.random.fold_in(key, 11)
    key_scale, key_value = jax.random.split(key)
    position = (jnp.arange(FEATS) % B).astype(jnp.float32) / B
    jitter = jax.random.uniform(key_scale, (FEATS,), jnp.float32)
    values = jnp.clip(jax.random.normal(key_value, (TOKENS, FEATS), jnp.float32), -6.0, 6.0)
    scales = 3.0 ** (position - 0.5) * 10.0 ** (jitter - 0.5)
    return (values * scales[None, :]).astype(jnp.bfloat16)


def draw_dout(key, part):
    key = jax.random.fold_in(key, 12)
    key_scale, key_value = jax.random.split(key)
    factor = 0.3 / math.sqrt(TOKENS)
    position = jnp.arange(B).astype(jnp.float32) / B
    jitter = jax.random.uniform(key_scale, (BC, B), jnp.float32)
    values = jnp.clip(jax.random.normal(key_value, (TOKENS, BC, B), jnp.float32), -6.0, 6.0)
    scales = 3.0 ** (position[None, :] - 0.5) * 10.0 ** (jitter - 0.5)
    return (values * scales[None, :, :] * factor).astype(jnp.bfloat16)


def draw_left_root(key, part):
    key = jax.random.fold_in(key, 13)
    key_scale, key_value = jax.random.split(key)
    position = jnp.arange(B).astype(jnp.float32) / B
    jitter = jax.random.uniform(key_scale, (2 * NB, B), jnp.float32)
    identity = jnp.eye(B, dtype=jnp.float32)
    off_diagonal = 0.4 * jnp.clip(jax.random.normal(key_value, (2 * NB, B, B), jnp.float32), -6.0, 6.0)
    diagonal = 3.0 ** (position[None, :] - 0.5) * 10.0 ** (jitter - 0.5)
    unit_part = identity[None, :, :] + off_diagonal / math.sqrt(B)
    return (diagonal[:, :, None] * unit_part).astype(jnp.bfloat16)


def draw_right_root(key, part):
    key = jax.random.fold_in(key, 14)
    key_scale, key_value = jax.random.split(key)
    position = jnp.arange(B).astype(jnp.float32) / B
    jitter = jax.random.uniform(key_scale, (2 * NB, B), jnp.float32)
    identity = jnp.eye(B, dtype=jnp.float32)
    off_diagonal = 0.4 * jnp.clip(jax.random.normal(key_value, (2 * NB, B, B), jnp.float32), -6.0, 6.0)
    diagonal = 3.0 ** (position[None, :] - 0.5) * 10.0 ** (jitter - 0.5)
    unit_part = identity[None, :, :] + off_diagonal / math.sqrt(B)
    return (unit_part * diagonal[:, None, :]).astype(jnp.bfloat16)


def set_ends(values, own_key, low, top_value):
    longest = values.shape.index(max(values.shape))
    spots = []
    for shift in (0, 1):
        where = [jax.random.randint(jax.random.fold_in(own_key, axis), (), 0, length) for axis, length in enumerate(values.shape)]
        where[longest] = (where[longest] + shift) % values.shape[longest]
        spots.append(tuple(where))
    return values.at[spots[0]].set(low).at[spots[1]].set(top_value)


def shard_levels(stream_key, shape, pieces, smallest, high):
    def one(dim, blocks):
        heights = jax.random.uniform(jax.random.fold_in(jax.random.fold_in(stream_key, 6), dim), (blocks,), jnp.float32, smallest / len(pieces), high / len(pieces))
        return jnp.repeat(jnp.exp(heights), shape[dim] // blocks).reshape((-1,) + (1,) * (len(shape) - dim - 1))

    level = one(*pieces[0])
    for cut in pieces[1:]:
        level = level * one(*cut)
    return level


def assign_block(key, own, number, rows, count, top, bound, skew):
    ranking = jax.random.permutation(key, count)
    packed, ordinary = portions_of(count, rows * top, bound, skew, True), portions_of(count, rows * top, bound, skew, False)
    places = jnp.arange(count)

    def named(tallies, rotation):
        used = int((tallies > 0).sum())
        fixed = max(1, used // 4)
        passed = fixed + (places - fixed + rotation * (used - fixed)) % max(1, count - fixed)
        return jnp.zeros((count,), jnp.int32).at[ranking[jnp.where(places < fixed, places, passed)]].set(jnp.asarray(tallies, jnp.int32))

    tallies = jnp.where(number % 4 == 0, named(packed, number // 4), named(ordinary, number - number // 4 - 1))
    mixed = jax.random.permutation(jax.random.fold_in(own, 3), count)
    giver, sink = mixed[0:count // 2 * 2:2], mixed[1:count // 2 * 2:2]
    slack = jnp.minimum(tallies[giver] - 1, bound - tallies[sink]) // 2
    slack = jnp.where((giver == ranking[0]) | (sink == ranking[0]) | (tallies[sink] == 0), 0, jnp.maximum(slack, 0))
    passed = jax.random.randint(jax.random.fold_in(own, 4), (count // 2,), 0, 1 << 20) % (slack + 1)
    tallies = tallies.at[giver].add(-passed).at[sink].add(passed)
    labels = jnp.searchsorted(jnp.cumsum(tallies), jnp.arange(rows * top), side="right").astype(jnp.int32)
    listing = labels.reshape(top, rows).T
    listing = listing[jax.random.permutation(jax.random.fold_in(own, 1), rows)]
    rotation = jax.random.randint(jax.random.fold_in(own, 2), (rows, 1), 0, top)
    return jnp.take_along_axis(listing, (jnp.arange(top)[None, :] + rotation) % top, axis=1)


def portions_of(count, total, reach, lean, full):
    loads = [(1 << 20) // math.isqrt(rank ** lean) + 1 for rank in range(1, count + 1)]
    largest = reach if full else min(reach, max(-(-total // count), total * loads[0] // sum(loads)))
    least = 1 if total - largest >= count - 1 else 0
    holding, rest = [largest] + [least] * (count - 1), total - largest - least * (count - 1)
    while rest > 0:
        free = [i for i in range(1, count) if holding[i] < largest] or [i for i in range(1, count) if holding[i] < reach]
        pool, remaining = sum([loads[i] for i in free]), rest
        for i in free:
            extra = min(reach - holding[i], max(1, remaining * loads[i] // pool), rest)
            holding[i] = holding[i] + extra
            rest = rest - extra
    return np.array(holding)


def centred(rng, shape, deviation, limit, cuts=(), kind=jnp.bfloat16):
    result = deviation * jax.random.normal(rng, shape, jnp.float32)
    if cuts:
        result = result * shard_levels(rng, shape, cuts, -0.22, 0.18)
    return jnp.clip(result, -limit, limit).astype(kind)


def setup_inputs(seed: int = 0) -> dict:
    arg_keys = jax.random.split(jax.random.key(seed), 9)
    acts = draw_acts(jax.random.fold_in(arg_keys[8], 71), 0)
    dout = draw_dout(jax.random.fold_in(arg_keys[8], 71), 0)
    left_stats = centred(arg_keys[2], (N_OWNER * SLOTS, B, B), 0.5, 3.0, ((0, 32), (1, 32)), jnp.float32)
    right_stats = centred(arg_keys[3], (N_OWNER * SLOTS, B, B), 0.5, 3.0, ((0, 32), (1, 32)), jnp.float32)
    left_root = draw_left_root(jax.random.fold_in(arg_keys[8], 71), 0)
    right_root = draw_right_root(jax.random.fold_in(arg_keys[8], 71), 0)
    owner_of_keys = jax.random.split(jax.random.fold_in(arg_keys[6], 1), NB // NB)
    owner_of_turns = jax.random.permutation(jax.random.fold_in(arg_keys[6], 3), NB // NB)
    owner_of = jax.vmap(lambda own, number: assign_block(jax.random.fold_in(arg_keys[6], 2), own, number, NB, N_OWNER, 1, SLOTS, 2))(owner_of_keys, owner_of_turns).reshape((NB, 1))
    counters = set_ends(jax.random.randint(arg_keys[7], (NB,), 0, 2 * WARMUP), jax.random.fold_in(arg_keys[7], 1), 0, (2 * WARMUP) - 1).astype(jnp.int32)
    return {"acts": acts, "dout": dout, "left_stats": left_stats, "right_stats": right_stats, "left_root": left_root, "right_root": right_root, "owner_of": owner_of, "counters": counters}


decay_rate = 0.95
epsilon = 1e-06

def slot_table(owner_of):
    owners = owner_of[:, 0].astype(jnp.int32)
    total = owners.shape[0]
    same_owner = owners[None, :] == owners[:, None]
    ordinal = jnp.arange(total, dtype=jnp.int32)
    earlier = ordinal[None, :] < ordinal[:, None]
    return (owners, lax.optimization_barrier(jnp.sum((same_owner & earlier).astype(jnp.int32), axis=1)).astype(jnp.int32))

def reference(acts, dout, left_stats, right_stats, left_root, right_root, owner_of, counters):
    flat_dout = dout.reshape(TOKENS, D)
    gradient = jnp.dot(acts.T, flat_dout, preferred_element_type=jnp.float32).astype(jnp.bfloat16)
    grad_block = gradient.reshape(BR, B, BC, B).transpose(0, 2, 1, 3).reshape(NB, B, B)
    owners, slot_of = slot_table(owner_of)
    place = (owners * SLOTS + slot_of).astype(jnp.int32)
    slot_grad = jnp.zeros((N_OWNER * SLOTS, B, B), jnp.bfloat16).at[place].set(grad_block)
    grad_wide = slot_grad.astype(jnp.float32)
    highest = lax.Precision.HIGHEST
    left_prod = jnp.einsum('sik,sjk->sij', grad_wide, grad_wide, precision=highest)
    right_prod = jnp.einsum('ski,skj->sij', grad_wide, grad_wide, precision=highest)
    left_out = decay_rate * left_stats + (1.0 - decay_rate) * left_prod
    right_out = decay_rate * right_stats + (1.0 - decay_rate) * right_prod
    inner = jnp.einsum('sik,skj->sij', left_root.astype(jnp.float32), grad_wide, precision=highest).astype(jnp.bfloat16)
    precond = jnp.einsum('sik,skj->sij', inner.astype(jnp.float32), right_root.astype(jnp.float32), precision=highest).astype(jnp.bfloat16)
    precise = precond.astype(jnp.float32)
    grad_sq = lax.optimization_barrier(jnp.sum(grad_wide * grad_wide, axis=(1, 2)))
    pre_sq = lax.optimization_barrier(jnp.sum(precise * precise, axis=(1, 2)))
    graft = jnp.sqrt(grad_sq / (pre_sq + epsilon))
    scaled = (precise * graft[:, None, None]).astype(jnp.bfloat16)
    started = counters >= WARMUP
    block_update = jnp.where(started[:, None, None], scaled[place], grad_block)
    update = block_update.reshape(BR, BC, B, B).transpose(0, 2, 1, 3)
    return (left_out, right_out, update)
```

```python
import functools

import jax
import jax.numpy as jnp
from jax import lax
from jax.experimental import pallas as pl
from jax.experimental.pallas import tpu as pltpu
from jax.sharding import PartitionSpec as P

WARMUP = 25
MESH = pl.DeviceIdType.MESH
LANES = 128
RING_GROUPS = 2
STOP = {1: 0, 2: 1, 3: 0, 4: 3, 5: 3, 6: 0, 7: 6, 8: 6}

decay_rate = 0.95
epsilon = 1e-06


def far_first(k, size):
    odd = lax.rem(k, 2)
    return lax.rem(size // 2 + size + odd * ((k + 1) // 2) - (1 - odd) * (k // 2), size)


def place_tables(owner_row, counter_row, slot_count, col_blocks):
    total = owner_row.shape[1]
    square = (total, total)
    down = lax.broadcasted_iota(jnp.int32, square, 0)
    across = lax.broadcasted_iota(jnp.int32, square, 1)

    def upright(row):
        return jnp.sum(jnp.where(down == across, row, 0), axis=1, keepdims=True)

    owner_col, counter_col = upright(owner_row), upright(counter_row)
    same = owner_col == owner_row
    slot_col = jnp.sum(jnp.where(same & (across < down), 1, 0), axis=1, keepdims=True)
    slot_row = jnp.sum(jnp.where(same & (down < across), 1, 0), axis=0, keepdims=True)
    block_col, block_row = down[:, :1], across[:1, :]
    last = col_blocks - 1
    taken = (block_col & ~last) + ((slot_col - block_col) & last)
    given = owner_row * col_blocks + ((block_row - slot_row) & last)
    places = lax.broadcasted_iota(jnp.int32, (total, LANES), 1)
    hit = owner_col * slot_count + slot_col == places
    source = total + jnp.sum(jnp.where(hit, taken - total, 0), axis=0, keepdims=True)
    begun = jnp.sum(jnp.where(hit & (counter_col >= WARMUP), 1, 0), axis=0, keepdims=True)
    return source, given, begun


def step_kernel(
    owner_hbm,
    counter_hbm,
    dout_hbm,
    acts_hbm,
    left_root_hbm,
    right_root_hbm,
    left_prod,
    right_prod,
    update,
    owner_v,
    counter_v,
    table_v,
    table,
    acts_v,
    dout_v,
    left_root,
    roots,
    right_root,
    terms,
    sibling_terms,
    sum_out,
    sum_in,
    turned,
    tile_out,
    tile_in,
    own_grad,
    grads,
    flipped,
    pre_out,
    precond,
    prod_out,
    prod_in,
    norm_out,
    norm_in,
    pre_tiles,
    grad_tiles,
    result_out,
    result_in,
    returned,
    acts_sem,
    load_sem,
    pair_send,
    pair_recv,
    ring_send,
    ring_recv,
    tile_send,
    tile_recv,
    gather_send,
    gather_recv,
    swap_send,
    swap_recv,
    norm_send,
    norm_recv,
    result_send,
    result_recv,
):
    replica = lax.axis_index("dp")
    owner = lax.axis_index("owner")
    replicas = grads.shape[0]
    owners = tile_in.shape[0]
    chips = replicas // 2
    half = chips // 2
    chip = replica // 2
    core = lax.rem(replica, 2)
    row_blocks, tokens, order = acts_v.shape
    slots, rows, _ = own_grad.shape
    col_blocks = turned.shape[0] // row_blocks
    share = LANES // col_blocks
    group_rows = row_blocks // RING_GROUPS
    kept = slots // 2
    mine = pl.ds(core * kept, kept)
    theirs = pl.ds((1 - core) * kept, kept)
    f32, bf16 = jnp.float32, jnp.bfloat16

    def acts_copy(i):
        return pltpu.make_async_copy(
            acts_hbm.at[:, pl.ds(pl.multiple_of(i * order, order), order)],
            acts_v.at[i],
            acts_sem.at[i],
        )

    dout_copy = pltpu.make_async_copy(dout_hbm, dout_v, load_sem.at[0])
    left_copy = pltpu.make_async_copy(left_root_hbm, left_root, load_sem.at[1])
    right_copy = pltpu.make_async_copy(right_root_hbm.at[mine], right_root, load_sem.at[2])
    owner_copy = pltpu.make_async_copy(owner_hbm, owner_v, load_sem.at[3])
    counter_copy = pltpu.make_async_copy(counter_hbm, counter_v, load_sem.at[4])
    table_copy = pltpu.make_async_copy(table_v, table, load_sem.at[5])
    owner_copy.start()
    counter_copy.start()
    dout_copy.start()
    for i in range(row_blocks):
        acts_copy(i).start()
    left_copy.start()
    right_copy.start()

    across = min(4, owners)

    def owner_peer(k):
        along = far_first(k // across, owners // across)
        aside = far_first(lax.rem(k, across), across)
        y = lax.rem(owner // across + along, owners // across)
        return y * across + lax.rem(lax.rem(owner, across) + aside, across)

    def replica_peer(k):
        there = lax.rem(chip + far_first(k // 2, chips), chips)
        return there * 2 + lax.rem(core + 1 - lax.rem(k, 2), 2)

    barrier = pltpu.get_barrier_semaphore()

    def greet_owner(k, carry):
        peer = owner_peer(k)
        pl.semaphore_signal(barrier, inc=1, device_id=(replica, peer), device_id_type=MESH)
        return carry

    def greet_replica(k, carry):
        peer = replica_peer(k)
        pl.semaphore_signal(barrier, inc=1, device_id=(peer, owner), device_id_type=MESH)
        return carry

    lax.fori_loop(0, replicas - 1, greet_replica, 0)
    lax.fori_loop(0, owners - 1, greet_owner, 0)
    turned[row_blocks * col_blocks] = jnp.zeros((rows, LANES), f32)
    owner_copy.wait()
    counter_copy.wait()
    source, given, begun = place_tables(owner_v[...], counter_v[...], slots, col_blocks)
    table_v[0:1, :] = source
    table_v[1:2, 0 : row_blocks * col_blocks] = given
    table_v[2:3, :] = begun
    table_copy.start()
    dout_copy.wait()

    sibling = (chip * 2 + 1 - core, owner)
    up = (lax.rem(chip + 1, chips) * 2 + core, owner)
    down = (lax.rem(chip + chips - 1, chips) * 2 + core, owner)

    def pair_copy(i):
        return pltpu.make_async_remote_copy(
            src_ref=terms.at[i, :, 1 - core],
            dst_ref=sibling_terms.at[i],
            send_sem=pair_send.at[i],
            recv_sem=pair_recv.at[i],
            device_id=sibling,
            device_id_type=MESH,
        )

    def term_step(i, carry):
        acts_copy(i).wait()
        part = jnp.dot(dout_v[...], acts_v[i], preferred_element_type=f32)
        terms[i] = part.T.astype(bf16).reshape(chips, 2, rows, LANES)
        return carry

    lax.fori_loop(0, row_blocks, term_step, 0)
    pl.semaphore_wait(barrier, owners + replicas - 2)
    for i in range(row_blocks):
        pair_copy(i).start()

    def swap_copy(which, source, target):
        return pltpu.make_async_remote_copy(
            src_ref=source,
            dst_ref=target,
            send_sem=swap_send.at[which],
            recv_sem=swap_recv.at[which],
            device_id=sibling,
            device_id_type=MESH,
        )

    root_swap = swap_copy(0, left_root.at[theirs], roots.at[core])
    grad_swap = swap_copy(1, own_grad.at[theirs], grads.at[replica])
    pre_swap = swap_copy(2, pre_out.at[1 - core], precond.at[mine])
    prod_swap = swap_copy(3, prod_out.at[1 - core], prod_in)
    left_copy.wait()
    root_swap.start()
    roots[core] = left_root[mine]

    def sum_copy(way, group, hops):
        step = hops - STOP[hops]
        peer = lax.rem(chip + (chips - step if way else step), chips) * 2 + core
        return pltpu.make_async_remote_copy(
            src_ref=sum_out.at[way, group, hops],
            dst_ref=sum_in.at[way, group, hops],
            send_sem=ring_send.at[way, group, hops],
            recv_sem=ring_recv.at[way, group, hops],
            device_id=(peer, owner),
            device_id_type=MESH,
        )

    def chip_terms(group, piece):
        here = pl.ds(group * group_rows, group_rows)
        return terms[here, piece, core].astype(f32) + sibling_terms[here, piece].astype(f32)

    def arrived(way, group, hops):
        sum_copy(way, group, hops).wait_recv()
        return sum_in[way, group, hops].astype(f32)

    def pass_on(way, group, hops):
        total = chip_terms(group, lax.rem(chip + (chips - hops if way else hops), chips))
        for other in routes[way]:
            if STOP[other] == hops:
                total = total + arrived(way, group, other)
        sum_out[way, group, hops] = total.astype(bf16)
        sum_copy(way, group, hops).start()

    routes = [range(1, half + 1), range(1, half)]
    for group in range(RING_GROUPS):
        for i in range(group * group_rows, (group + 1) * group_rows):
            pair_copy(i).wait_recv()
        for hops in range(half, 0, -1):
            for way in range(2):
                if hops in routes[way] and STOP[hops]:
                    pass_on(way, group, hops)
    for group in range(RING_GROUPS):
        for hops in range(half, 0, -1):
            for way in range(2):
                if hops in routes[way] and not STOP[hops]:
                    pass_on(way, group, hops)

    for group in range(RING_GROUPS):
        total = chip_terms(group, chip)
        for hops in range(1, half + 1):
            for way in range(2):
                if hops in routes[way] and not STOP[hops]:
                    total = total + arrived(way, group, hops)
        total = total.astype(bf16).astype(f32)
        for i in range(group_rows):
            for k in range(col_blocks):
                tile = total[i] if k == 0 else pltpu.roll(total[i], k * share, 1)
                turned[(group * group_rows + i) * col_blocks + k] = tile

    lane_block = lax.broadcasted_iota(jnp.int32, (rows, LANES), 1) // share

    table_copy.wait()

    def tile_copy(peer):
        return pltpu.make_async_remote_copy(
            src_ref=tile_out.at[peer],
            dst_ref=tile_in.at[owner],
            send_sem=tile_send,
            recv_sem=tile_recv,
            device_id=(replica, peer),
            device_id_type=MESH,
        )

    def tiles_for(peer):
        tile = jnp.zeros((rows, LANES), f32)
        for s in range(slots):
            tile = jnp.where(lane_block == s, turned[table[0, peer * slots + s]], tile)
        return tile.astype(bf16)

    def tile_step(k, carry):
        peer = owner_peer(k)
        tile_out[peer] = tiles_for(peer)
        tile_copy(peer).start()
        return carry

    lax.fori_loop(0, owners - 1, tile_step, 0)
    tile_in[owner] = tiles_for(owner)
    others = pl.ds(0, owners - 1)
    pltpu.make_async_copy(tile_in.at[others], tile_in.at[others], tile_recv).wait()

    pieces = [tile_in[o].astype(f32) for o in range(owners)]
    for s in range(slots):
        for q in range(order // LANES):
            tile = jnp.zeros((rows, LANES), f32)
            for k in range(col_blocks):
                shift = (k - s) * share % LANES
                piece = pieces[q * col_blocks + k]
                piece = pltpu.roll(piece, shift, 1) if shift else piece
                tile = jnp.where(lane_block == k, piece, tile)
            own_grad[s, :, q * LANES : (q + 1) * LANES] = tile.astype(bf16)
    grad_swap.start()
    grads[replica] = own_grad[mine]

    def gather_copy(way, step):
        there = lax.rem(chip + step if way else chip + chips - step, chips)
        piece = grads.at[pl.ds(there * 2, 2)]
        return pltpu.make_async_remote_copy(
            src_ref=piece,
            dst_ref=piece,
            send_sem=gather_send.at[way, step],
            recv_sem=gather_recv.at[way, step],
            device_id=down if way else up,
            device_id_type=MESH,
        )

    grad_swap.wait_recv()
    gather_copy(0, 0).start()
    if half > 1:
        gather_copy(1, 0).start()

    def gather_round(step, carry):
        for way in range(2):
            gather_copy(way, step - 1).wait_recv()
            gather_copy(way, step).start()
        return carry

    lax.fori_loop(1, half - 1, gather_round, 0)
    if half > 1:
        gather_copy(0, half - 2).wait_recv()
        gather_copy(0, half - 1).start()
    root_swap.wait_recv()
    right_copy.wait()
    if half > 1:
        gather_copy(1, half - 2).wait_recv()
    gather_copy(0, half - 1).wait_recv()

    lane = lax.broadcasted_iota(jnp.int32, (1, LANES), 1)
    norms = jnp.zeros((1, LANES), f32)
    for t in range(kept):
        whole = grads[:, t].reshape(order, order)
        root = roots[:, t].reshape(2 * rows, order)
        inner = jnp.dot(root, whole, preferred_element_type=f32).astype(bf16)
        pre = jnp.dot(inner, right_root[t], preferred_element_type=f32).astype(bf16)
        pre_out[:, t] = pre.reshape(2, rows, order)
        pre = pre.astype(f32)
        square = jnp.sum(pre * pre, axis=(0, 1), keepdims=True)
        norms = jnp.where(lane == core * kept + t, square, norms)
    for s in range(slots):
        own = own_grad[s].astype(f32)
        square = jnp.sum(own * own, axis=(0, 1), keepdims=True)
        norms = jnp.where(lane == slots + s, square, norms)
    norm_out[...] = norms

    def norm_copy(peer):
        return pltpu.make_async_remote_copy(
            src_ref=norm_out,
            dst_ref=norm_in.at[replica],
            send_sem=norm_send,
            recv_sem=norm_recv,
            device_id=(peer, owner),
            device_id_type=MESH,
        )

    def norm_step(k, carry):
        norm_copy(replica_peer(k)).start()
        return carry

    lax.fori_loop(0, replicas - 1, norm_step, 0)
    pre_swap.start()
    norm_in[replica] = norms
    precond[mine] = pre_out[core]
    pre_swap.wait_recv()

    for q in range(order // LANES):
        here = slice(q * LANES, (q + 1) * LANES)
        pre_parts = [precond[s, :, here].astype(f32) for s in range(slots)]
        own_parts = [own_grad[s, :, here].astype(f32) for s in range(slots)]
        for k in range(col_blocks):
            pre_tile = jnp.zeros((rows, LANES), f32)
            own_tile = jnp.zeros((rows, LANES), f32)
            for s in range(slots):
                shift = (s - k) * share % LANES
                pre_part, own_part = pre_parts[s], own_parts[s]
                if shift:
                    pre_part = pltpu.roll(pre_part, shift, 1)
                    own_part = pltpu.roll(own_part, shift, 1)
                pre_tile = jnp.where(lane_block == s, pre_part, pre_tile)
                own_tile = jnp.where(lane_block == s, own_part, own_tile)
            pre_tiles[q * col_blocks + k] = pre_tile
            grad_tiles[q * col_blocks + k] = own_tile

    other_replicas = pl.ds(0, replicas - 1)
    pltpu.make_async_copy(
        norm_in.at[other_replicas], norm_in.at[other_replicas], norm_recv
    ).wait()
    norms = jnp.sum(norm_in[...], axis=0)
    scale = jnp.zeros((1, LANES), f32)
    started = jnp.zeros((1, LANES), jnp.int32)
    for s in range(slots):
        graft = jnp.sqrt(norms[:, slots + s : slots + s + 1] / (norms[:, s : s + 1] + epsilon))
        scale = jnp.where(lane // share == s, graft, scale)
        started = jnp.where(lane // share == s, table[2, owner * slots + s], started)

    def result_copy(peer):
        return pltpu.make_async_remote_copy(
            src_ref=result_out.at[peer],
            dst_ref=result_in.at[owner],
            send_sem=result_send,
            recv_sem=result_recv,
            device_id=(replica, peer),
            device_id_type=MESH,
        )

    def result_for(peer):
        return jnp.where(started > 0, pre_tiles[peer] * scale, grad_tiles[peer]).astype(bf16)

    def result_step(k, carry):
        peer = owner_peer(k)
        result_out[peer] = result_for(peer)
        result_copy(peer).start()
        return carry

    lax.fori_loop(0, owners - 1, result_step, 0)
    result_in[owner] = result_for(owner)

    span = pl.ds(pl.multiple_of(chip * 2 * rows // LANES * LANES, LANES), LANES)
    for t in range(kept):
        whole = grads[:, t].reshape(order, order)
        both = grads[pl.ds(chip * 2, 2), t].reshape(2 * rows, order)
        left = lax.dot_general(
            both, whole, (((1,), (1,)), ((), ())), preferred_element_type=f32
        )
        columns = grads[:, t, :, span].reshape(order, LANES)
        flipped[t] = columns.T.reshape(LANES // (2 * rows), 2 * rows, order)
        turned_rows = flipped[t, lax.rem(chip, LANES // (2 * rows))]
        right = jnp.dot(turned_rows, whole, preferred_element_type=f32)
        prod_out[:, 0, t] = left.reshape(2, rows, order)
        prod_out[:, 1, t] = right.reshape(2, rows, order)
    prod_swap.start()
    left_prod[mine] = prod_out[core, 0]
    right_prod[mine] = prod_out[core, 1]

    pltpu.make_async_copy(result_in.at[others], result_in.at[others], result_recv).wait()

    def turn_step(o, carry):
        tile = result_in[o].astype(f32)
        for k in range(col_blocks):
            returned[o * col_blocks + k] = pltpu.roll(tile, k * share, 1) if k else tile
        return carry

    lax.fori_loop(0, owners, turn_step, 0)

    def update_step(i, carry):
        tile = jnp.zeros((rows, LANES), f32)
        for j in range(col_blocks):
            tile = jnp.where(lane_block == j, returned[table[1, i * col_blocks + j]], tile)
        update[i] = tile.astype(bf16)
        return carry

    lax.fori_loop(0, row_blocks, update_step, 0)

    prod_swap.wait_recv()
    left_prod[theirs] = prod_in[0]
    right_prod[theirs] = prod_in[1]

    root_swap.wait_send()
    grad_swap.wait_send()
    pre_swap.wait_send()
    prod_swap.wait_send()
    for i in range(row_blocks):
        pair_copy(i).wait_send()

    def sent(step, carry):
        for way in range(2):
            gather_copy(way, step).wait_send()
        return carry

    lax.fori_loop(0, half - 1, sent, 0)
    for way in range(2):
        for group in range(RING_GROUPS):
            for hops in routes[way]:
                sum_copy(way, group, hops).wait_send()
    gather_copy(0, half - 1).wait_send()
    pltpu.make_async_copy(tile_in.at[others], tile_in.at[others], tile_send).wait()
    pltpu.make_async_copy(
        norm_in.at[other_replicas], norm_in.at[other_replicas], norm_send
    ).wait()
    pltpu.make_async_copy(result_in.at[others], result_in.at[others], result_send).wait()


def finish_kernel(
    left_stats,
    right_stats,
    left_prod,
    right_prod,
    tiles,
    left_out,
    right_out,
    update,
    left_v,
    right_v,
    left_prod_v,
    right_prod_v,
    tiles_v,
    load_sem,
):
    col_blocks, share = update.shape[2:]
    sources = (tiles, left_stats, left_prod, right_stats, right_prod)
    targets = (tiles_v, left_v, left_prod_v, right_v, right_prod_v)
    copies = [
        pltpu.make_async_copy(source, target, load_sem.at[i])
        for i, (source, target) in enumerate(zip(sources, targets))
    ]
    for copy in copies:
        copy.start()
    copies[0].wait()
    for j in range(col_blocks):
        update[:, :, j, :] = tiles_v[:, :, j * share : (j + 1) * share]
    copies[1].wait()
    copies[2].wait()
    left_out[...] = decay_rate * left_v[...] + (1.0 - decay_rate) * left_prod_v[...]
    copies[3].wait()
    copies[4].wait()
    right_out[...] = decay_rate * right_v[...] + (1.0 - decay_rate) * right_prod_v[...]


def on_device(acts, dout, left_stats, right_stats, left_root, right_root, owner_of, counters):
    replicas, owners = lax.axis_size("dp"), lax.axis_size("owner")
    tokens, features = acts.shape
    col_blocks, share = dout.shape[1:]
    slots, rows, order = left_stats.shape
    row_blocks = features // order
    chips = replicas // 2
    half = chips // 2
    f32, bf16 = jnp.float32, jnp.bfloat16
    total = counters.shape[0]
    dout_rows = dout.transpose(1, 2, 0).reshape(col_blocks * share, tokens)
    vmem = functools.partial(pl.BlockSpec, memory_space=pltpu.VMEM)
    anywhere = functools.partial(pl.BlockSpec, memory_space=pl.ANY)
    kept = slots // 2
    ring_shape = (2, RING_GROUPS, half + 1, row_blocks // RING_GROUPS, rows, LANES)
    dma = pltpu.SemaphoreType.DMA
    left_prod, right_prod, update = pl.pallas_call(
        step_kernel,
        out_shape=(
            jax.ShapeDtypeStruct((slots, rows, order), f32),
            jax.ShapeDtypeStruct((slots, rows, order), f32),
            jax.ShapeDtypeStruct((row_blocks, rows, LANES), bf16),
        ),
        in_specs=[anywhere()] * 6,
        out_specs=(vmem(), vmem(), vmem()),
        scratch_shapes=[
            pltpu.VMEM((1, total), jnp.int32),
            pltpu.VMEM((1, total), jnp.int32),
            pltpu.VMEM((8, LANES), jnp.int32),
            pltpu.SMEM((8, LANES), jnp.int32),
            pltpu.VMEM((row_blocks, tokens, order), bf16),
            pltpu.VMEM((LANES, tokens), bf16),
            pltpu.VMEM((slots, rows, order), bf16),
            pltpu.VMEM((2, kept, rows, order), bf16),
            pltpu.VMEM((kept, order, order), bf16),
            pltpu.VMEM((row_blocks, chips, 2, rows, LANES), bf16),
            pltpu.VMEM((row_blocks, chips, rows, LANES), bf16),
            pltpu.VMEM(ring_shape, bf16),
            pltpu.VMEM(ring_shape, bf16),
            pltpu.VMEM((row_blocks * col_blocks + 1, rows, LANES), f32),
            pltpu.VMEM((owners, rows, LANES), bf16),
            pltpu.VMEM((owners, rows, LANES), bf16),
            pltpu.VMEM((slots, rows, order), bf16),
            pltpu.VMEM((replicas, kept, rows, order), bf16),
            pltpu.VMEM((kept, LANES // (2 * rows), 2 * rows, order), bf16),
            pltpu.VMEM((2, kept, rows, order), bf16),
            pltpu.VMEM((slots, rows, order), bf16),
            pltpu.VMEM((2, 2, kept, rows, order), f32),
            pltpu.VMEM((2, kept, rows, order), f32),
            pltpu.VMEM((1, LANES), f32),
            pltpu.VMEM((replicas, 1, LANES), f32),
            pltpu.VMEM((owners, rows, LANES), f32),
            pltpu.VMEM((owners, rows, LANES), f32),
            pltpu.VMEM((owners, rows, LANES), bf16),
            pltpu.VMEM((owners, rows, LANES), bf16),
            pltpu.VMEM((owners * col_blocks, rows, LANES), f32),
            dma((row_blocks,)),
            dma((6,)),
            dma((row_blocks,)),
            dma((row_blocks,)),
            dma((2, RING_GROUPS, half + 1)),
            dma((2, RING_GROUPS, half + 1)),
            dma,
            dma,
            dma((2, half)),
            dma((2, half)),
            dma((4,)),
            dma((4,)),
            dma,
            dma,
            dma,
            dma,
        ],
        compiler_params=pltpu.CompilerParams(
            collective_id=0, has_side_effects=True, vmem_limit_bytes=56 * 1024 * 1024
        ),
    )(owner_of.reshape(1, total), counters.reshape(1, total), dout_rows, acts, left_root, right_root)
    return pl.pallas_call(
        finish_kernel,
        out_shape=(
            jax.ShapeDtypeStruct((slots, rows, order), f32),
            jax.ShapeDtypeStruct((slots, rows, order), f32),
            jax.ShapeDtypeStruct((row_blocks, rows, col_blocks, share), bf16),
        ),
        in_specs=[anywhere()] * 5,
        out_specs=(vmem(), vmem(), vmem()),
        scratch_shapes=[pltpu.VMEM((slots, rows, order), f32)] * 4
        + [pltpu.VMEM((row_blocks, rows, LANES), bf16), dma((5,))],
    )(left_stats, right_stats, left_prod, right_prod, update)


def solution(mesh):
    in_specs = (
        P("dp", None),
        P("dp", None, "owner"),
        P("owner", "dp", None),
        P("owner", "dp", None),
        P("owner", "dp", None),
        P("owner", None, None),
        P(),
        P(),
    )
    out_specs = (P("owner", "dp", None), P("owner", "dp", None), P(None, "dp", None, "owner"))
    return jax.shard_map(
        on_device, mesh=mesh, in_specs=in_specs, out_specs=out_specs, check_vma=False
    )
```

```python
import functools

import jax
import jax.numpy as jnp
from jax import lax
from jax.experimental import pallas as pl
from jax.experimental.pallas import tpu as pltpu
from jax.sharding import PartitionSpec as P

WARMUP = 25
MESH = pl.DeviceIdType.MESH
LANES = 128
RING_GROUPS = 2
STOP = {1: 0, 2: 1, 3: 0, 4: 3, 5: 3, 6: 0, 7: 6, 8: 6}

decay_rate = 0.95
epsilon = 1e-06


def around(place, size):
    place = jnp.where(place >= size, place - size, place)
    return jnp.where(place < 0, place + size, place)


def far_first(size):
    return [(size // 2 + ((k + 1) // 2 if k % 2 else -(k // 2))) % size for k in range(size)]


def swing(size, visit):
    def step(k, carry):
        distance, stride, side = carry
        visit(distance)
        return distance + side * stride, stride + 1, -side

    lax.fori_loop(0, size - 1, step, (jnp.int32(size // 2), jnp.int32(1), jnp.int32(1)))


def place_tables(owner_row, counter_row, slot_count, col_blocks):
    total = owner_row.shape[1]
    square = (total, total)
    down = lax.broadcasted_iota(jnp.int32, square, 0)
    across = lax.broadcasted_iota(jnp.int32, square, 1)

    def upright(row):
        return jnp.sum(jnp.where(down == across, row, 0), axis=1, keepdims=True)

    owner_col, counter_col = upright(owner_row), upright(counter_row)
    same = owner_col == owner_row
    slot_col = jnp.sum(jnp.where(same & (across < down), 1, 0), axis=1, keepdims=True)
    slot_row = jnp.sum(jnp.where(same & (down < across), 1, 0), axis=0, keepdims=True)
    block_col, block_row = down[:, :1], across[:1, :]
    last = col_blocks - 1
    taken = (block_col & ~last) + ((slot_col - block_col) & last)
    given = owner_row * col_blocks + ((block_row - slot_row) & last)
    places = lax.broadcasted_iota(jnp.int32, (total, LANES), 1)
    hit = owner_col * slot_count + slot_col == places
    source = total + jnp.sum(jnp.where(hit, taken - total, 0), axis=0, keepdims=True)
    begun = jnp.sum(jnp.where(hit & (counter_col >= WARMUP), 1, 0), axis=0, keepdims=True)
    return source, given, begun


def step_kernel(
    owner_hbm,
    counter_hbm,
    dout_hbm,
    acts_hbm,
    left_root_hbm,
    right_root_hbm,
    left_prod,
    right_prod,
    update,
    owner_v,
    counter_v,
    table_v,
    table,
    acts_v,
    dout_v,
    left_root,
    roots,
    right_root,
    terms,
    sibling_terms,
    sum_out,
    sum_in,
    turned,
    tile_out,
    tile_in,
    own_grad,
    grads,
    flipped,
    pre_out,
    precond,
    prod_out,
    prod_in,
    norm_out,
    norm_in,
    pre_tiles,
    grad_tiles,
    result_out,
    result_in,
    returned,
    acts_sem,
    load_sem,
    pair_send,
    pair_recv,
    ring_send,
    ring_recv,
    tile_send,
    tile_recv,
    gather_send,
    gather_recv,
    swap_send,
    swap_recv,
    norm_send,
    norm_recv,
    result_send,
    result_recv,
):
    replica = lax.axis_index("dp")
    owner = lax.axis_index("owner")
    replicas = grads.shape[0]
    owners = tile_in.shape[0]
    chips = replicas // 2
    half = chips // 2
    chip = replica // 2
    core = lax.rem(replica, 2)
    row_blocks, tokens, order = acts_v.shape
    slots, rows, _ = own_grad.shape
    col_blocks = turned.shape[0] // row_blocks
    share = LANES // col_blocks
    group_rows = row_blocks // RING_GROUPS
    kept = slots // 2
    mine = pl.ds(core * kept, kept)
    theirs = pl.ds((1 - core) * kept, kept)
    f32, bf16 = jnp.float32, jnp.bfloat16

    def acts_copy(i):
        return pltpu.make_async_copy(
            acts_hbm.at[:, pl.ds(pl.multiple_of(i * order, order), order)],
            acts_v.at[i],
            acts_sem.at[i],
        )

    dout_copy = pltpu.make_async_copy(dout_hbm, dout_v, load_sem.at[0])
    left_copy = pltpu.make_async_copy(left_root_hbm, left_root, load_sem.at[1])
    right_copy = pltpu.make_async_copy(right_root_hbm.at[mine], right_root, load_sem.at[2])
    owner_copy = pltpu.make_async_copy(owner_hbm, owner_v, load_sem.at[3])
    counter_copy = pltpu.make_async_copy(counter_hbm, counter_v, load_sem.at[4])
    table_copy = pltpu.make_async_copy(table_v, table, load_sem.at[5])
    owner_copy.start()
    counter_copy.start()
    dout_copy.start()
    for i in range(row_blocks):
        acts_copy(i).start()
    left_copy.start()
    right_copy.start()

    across = min(4, owners)

    high, wide = owner // across, lax.rem(owner, across)
    beside = [around(wide + d, across) for d in far_first(across)]

    def each_owner(visit):
        def row(distance):
            y = around(high + distance, owners // across) * across
            for x in beside:
                visit(y + x)

        swing(owners // across, row)
        for x in beside[:-1]:
            visit(high * across + x)

    def each_replica(visit):
        def both(distance):
            there = around(chip + distance, chips) * 2
            visit(there)
            visit(there + 1)

        swing(chips, both)
        visit(chip * 2 + 1 - core)

    barrier = pltpu.get_barrier_semaphore()

    def greet_owner(peer):
        pl.semaphore_signal(barrier, inc=1, device_id=(replica, peer), device_id_type=MESH)

    def greet_replica(peer):
        pl.semaphore_signal(barrier, inc=1, device_id=(peer, owner), device_id_type=MESH)

    each_replica(greet_replica)
    each_owner(greet_owner)
    turned[row_blocks * col_blocks] = jnp.zeros((rows, LANES), f32)
    owner_copy.wait()
    counter_copy.wait()
    source, given, begun = place_tables(owner_v[...], counter_v[...], slots, col_blocks)
    table_v[0:1, :] = source
    table_v[1:2, 0 : row_blocks * col_blocks] = given
    table_v[2:3, :] = begun
    table_copy.start()
    dout_copy.wait()

    sibling = (chip * 2 + 1 - core, owner)
    up = (around(chip + 1, chips) * 2 + core, owner)
    down = (around(chip - 1, chips) * 2 + core, owner)

    def pair_copy(i):
        return pltpu.make_async_remote_copy(
            src_ref=terms.at[i, :, 1 - core],
            dst_ref=sibling_terms.at[i],
            send_sem=pair_send.at[i],
            recv_sem=pair_recv.at[i],
            device_id=sibling,
            device_id_type=MESH,
        )

    def term_step(i, carry):
        acts_copy(i).wait()
        part = jnp.dot(dout_v[...], acts_v[i], preferred_element_type=f32)
        terms[i] = part.T.astype(bf16).reshape(chips, 2, rows, LANES)
        return carry

    lax.fori_loop(0, row_blocks, term_step, 0)
    pl.semaphore_wait(barrier, owners + replicas - 2)
    for i in range(row_blocks):
        pair_copy(i).start()

    def swap_copy(which, source, target):
        return pltpu.make_async_remote_copy(
            src_ref=source,
            dst_ref=target,
            send_sem=swap_send.at[which],
            recv_sem=swap_recv.at[which],
            device_id=sibling,
            device_id_type=MESH,
        )

    root_swap = swap_copy(0, left_root.at[theirs], roots.at[core])
    grad_swap = swap_copy(1, own_grad.at[theirs], grads.at[replica])
    pre_swap = swap_copy(2, pre_out.at[1 - core], precond.at[mine])
    prod_swap = swap_copy(3, prod_out.at[1 - core], prod_in)
    left_copy.wait()
    root_swap.start()
    roots[core] = left_root[mine]

    def sum_copy(way, group, hops):
        step = hops - STOP[hops]
        peer = around(chip + (-step if way else step), chips) * 2 + core
        return pltpu.make_async_remote_copy(
            src_ref=sum_out.at[way, group, hops],
            dst_ref=sum_in.at[way, group, hops],
            send_sem=ring_send.at[way, group, hops],
            recv_sem=ring_recv.at[way, group, hops],
            device_id=(peer, owner),
            device_id_type=MESH,
        )

    def chip_terms(group, piece):
        here = pl.ds(group * group_rows, group_rows)
        return terms[here, piece, core].astype(f32) + sibling_terms[here, piece].astype(f32)

    def arrived(way, group, hops):
        sum_copy(way, group, hops).wait_recv()
        return sum_in[way, group, hops].astype(f32)

    def pass_on(way, group, hops):
        total = chip_terms(group, around(chip + (-hops if way else hops), chips))
        for other in routes[way]:
            if STOP[other] == hops:
                total = total + arrived(way, group, other)
        sum_out[way, group, hops] = total.astype(bf16)
        sum_copy(way, group, hops).start()

    routes = [range(1, half + 1), range(1, half)]
    for group in range(RING_GROUPS):
        for i in range(group * group_rows, (group + 1) * group_rows):
            pair_copy(i).wait_recv()
        for hops in range(half, 0, -1):
            for way in range(2):
                if hops in routes[way] and STOP[hops]:
                    pass_on(way, group, hops)
    for group in range(RING_GROUPS):
        for hops in range(half, 0, -1):
            for way in range(2):
                if hops in routes[way] and not STOP[hops]:
                    pass_on(way, group, hops)

    for group in range(RING_GROUPS):
        total = chip_terms(group, chip)
        for hops in range(1, half + 1):
            for way in range(2):
                if hops in routes[way] and not STOP[hops]:
                    total = total + arrived(way, group, hops)
        total = total.astype(bf16).astype(f32)
        for i in range(group_rows):
            for k in range(col_blocks):
                tile = total[i] if k == 0 else pltpu.roll(total[i], k * share, 1)
                turned[(group * group_rows + i) * col_blocks + k] = tile

    lane_block = lax.broadcasted_iota(jnp.int32, (rows, LANES), 1) // share

    table_copy.wait()

    def tile_copy(peer):
        return pltpu.make_async_remote_copy(
            src_ref=tile_out.at[peer],
            dst_ref=tile_in.at[owner],
            send_sem=tile_send,
            recv_sem=tile_recv,
            device_id=(replica, peer),
            device_id_type=MESH,
        )

    def tiles_for(peer):
        tile = jnp.zeros((rows, LANES), f32)
        for s in range(slots):
            tile = jnp.where(lane_block == s, turned[table[0, peer * slots + s]], tile)
        return tile.astype(bf16)

    def tile_step(peer):
        tile_out[peer] = tiles_for(peer)
        tile_copy(peer).start()

    each_owner(tile_step)
    tile_in[owner] = tiles_for(owner)
    others = pl.ds(0, owners - 1)
    pltpu.make_async_copy(tile_in.at[others], tile_in.at[others], tile_recv).wait()

    pieces = [tile_in[o].astype(f32) for o in range(owners)]
    for s in range(slots):
        for q in range(order // LANES):
            tile = jnp.zeros((rows, LANES), f32)
            for k in range(col_blocks):
                shift = (k - s) * share % LANES
                piece = pieces[q * col_blocks + k]
                piece = pltpu.roll(piece, shift, 1) if shift else piece
                tile = jnp.where(lane_block == k, piece, tile)
            own_grad[s, :, q * LANES : (q + 1) * LANES] = tile.astype(bf16)
    grad_swap.start()
    grads[replica] = own_grad[mine]

    def gather_copy(way, step):
        there = around(chip + (step if way else -step), chips)
        piece = grads.at[pl.ds(there * 2, 2)]
        return pltpu.make_async_remote_copy(
            src_ref=piece,
            dst_ref=piece,
            send_sem=gather_send.at[way, step],
            recv_sem=gather_recv.at[way, step],
            device_id=down if way else up,
            device_id_type=MESH,
        )

    grad_swap.wait_recv()
    gather_copy(0, 0).start()
    if half > 1:
        gather_copy(1, 0).start()

    def gather_round(step, carry):
        for way in range(2):
            gather_copy(way, step - 1).wait_recv()
            gather_copy(way, step).start()
        return carry

    lax.fori_loop(1, half - 1, gather_round, 0)
    if half > 1:
        gather_copy(0, half - 2).wait_recv()
        gather_copy(0, half - 1).start()
    root_swap.wait_recv()
    right_copy.wait()
    if half > 1:
        gather_copy(1, half - 2).wait_recv()
    gather_copy(0, half - 1).wait_recv()

    lane = lax.broadcasted_iota(jnp.int32, (1, LANES), 1)
    norms = jnp.zeros((1, LANES), f32)
    for t in range(kept):
        whole = grads[:, t].reshape(order, order)
        root = roots[:, t].reshape(2 * rows, order)
        inner = jnp.dot(root, whole, preferred_element_type=f32).astype(bf16)
        pre = jnp.dot(inner, right_root[t], preferred_element_type=f32).astype(bf16)
        pre_out[:, t] = pre.reshape(2, rows, order)
        pre = pre.astype(f32)
        square = jnp.sum(pre * pre, axis=(0, 1), keepdims=True)
        norms = jnp.where(lane == core * kept + t, square, norms)
    for s in range(slots):
        own = own_grad[s].astype(f32)
        square = jnp.sum(own * own, axis=(0, 1), keepdims=True)
        norms = jnp.where(lane == slots + s, square, norms)
    norm_out[...] = norms

    def norm_copy(peer):
        return pltpu.make_async_remote_copy(
            src_ref=norm_out,
            dst_ref=norm_in.at[replica],
            send_sem=norm_send,
            recv_sem=norm_recv,
            device_id=(peer, owner),
            device_id_type=MESH,
        )

    def norm_step(peer):
        norm_copy(peer).start()

    each_replica(norm_step)
    pre_swap.start()
    norm_in[replica] = norms
    precond[mine] = pre_out[core]
    pre_swap.wait_recv()

    for q in range(order // LANES):
        here = slice(q * LANES, (q + 1) * LANES)
        pre_parts = [precond[s, :, here].astype(f32) for s in range(slots)]
        own_parts = [own_grad[s, :, here].astype(f32) for s in range(slots)]
        for k in range(col_blocks):
            pre_tile = jnp.zeros((rows, LANES), f32)
            own_tile = jnp.zeros((rows, LANES), f32)
            for s in range(slots):
                shift = (s - k) * share % LANES
                pre_part, own_part = pre_parts[s], own_parts[s]
                if shift:
                    pre_part = pltpu.roll(pre_part, shift, 1)
                    own_part = pltpu.roll(own_part, shift, 1)
                pre_tile = jnp.where(lane_block == s, pre_part, pre_tile)
                own_tile = jnp.where(lane_block == s, own_part, own_tile)
            pre_tiles[q * col_blocks + k] = pre_tile
            grad_tiles[q * col_blocks + k] = own_tile

    other_replicas = pl.ds(0, replicas - 1)
    pltpu.make_async_copy(
        norm_in.at[other_replicas], norm_in.at[other_replicas], norm_recv
    ).wait()
    norms = jnp.sum(norm_in[...], axis=0)
    scale = jnp.zeros((1, LANES), f32)
    started = jnp.zeros((1, LANES), jnp.int32)
    for s in range(slots):
        graft = jnp.sqrt(norms[:, slots + s : slots + s + 1] / (norms[:, s : s + 1] + epsilon))
        scale = jnp.where(lane // share == s, graft, scale)
        started = jnp.where(lane // share == s, table[2, owner * slots + s], started)

    def result_copy(peer):
        return pltpu.make_async_remote_copy(
            src_ref=result_out.at[peer],
            dst_ref=result_in.at[owner],
            send_sem=result_send,
            recv_sem=result_recv,
            device_id=(replica, peer),
            device_id_type=MESH,
        )

    def result_for(peer):
        return jnp.where(started > 0, pre_tiles[peer] * scale, grad_tiles[peer]).astype(bf16)

    def result_step(peer):
        result_out[peer] = result_for(peer)
        result_copy(peer).start()

    each_owner(result_step)
    result_in[owner] = result_for(owner)

    span = pl.ds(pl.multiple_of(chip * 2 * rows // LANES * LANES, LANES), LANES)
    for t in range(kept):
        whole = grads[:, t].reshape(order, order)
        both = grads[pl.ds(chip * 2, 2), t].reshape(2 * rows, order)
        left = lax.dot_general(
            both, whole, (((1,), (1,)), ((), ())), preferred_element_type=f32
        )
        columns = grads[:, t, :, span].reshape(order, LANES)
        flipped[t] = columns.T.reshape(LANES // (2 * rows), 2 * rows, order)
        turned_rows = flipped[t, lax.rem(chip, LANES // (2 * rows))]
        right = jnp.dot(turned_rows, whole, preferred_element_type=f32)
        prod_out[:, 0, t] = left.reshape(2, rows, order)
        prod_out[:, 1, t] = right.reshape(2, rows, order)
    prod_swap.start()
    left_prod[mine] = prod_out[core, 0]
    right_prod[mine] = prod_out[core, 1]

    pltpu.make_async_copy(result_in.at[others], result_in.at[others], result_recv).wait()

    def turn_step(o, carry):
        tile = result_in[o].astype(f32)
        for k in range(col_blocks):
            returned[o * col_blocks + k] = pltpu.roll(tile, k * share, 1) if k else tile
        return carry

    lax.fori_loop(0, owners, turn_step, 0)

    def update_step(i, carry):
        tile = jnp.zeros((rows, LANES), f32)
        for j in range(col_blocks):
            tile = jnp.where(lane_block == j, returned[table[1, i * col_blocks + j]], tile)
        update[i] = tile.astype(bf16)
        return carry

    lax.fori_loop(0, row_blocks, update_step, 0)

    prod_swap.wait_recv()
    left_prod[theirs] = prod_in[0]
    right_prod[theirs] = prod_in[1]

    root_swap.wait_send()
    grad_swap.wait_send()
    pre_swap.wait_send()
    prod_swap.wait_send()
    for i in range(row_blocks):
        pair_copy(i).wait_send()

    def sent(step, carry):
        for way in range(2):
            gather_copy(way, step).wait_send()
        return carry

    lax.fori_loop(0, half - 1, sent, 0)
    for way in range(2):
        for group in range(RING_GROUPS):
            for hops in routes[way]:
                sum_copy(way, group, hops).wait_send()
    gather_copy(0, half - 1).wait_send()
    pltpu.make_async_copy(tile_in.at[others], tile_in.at[others], tile_send).wait()
    pltpu.make_async_copy(
        norm_in.at[other_replicas], norm_in.at[other_replicas], norm_send
    ).wait()
    pltpu.make_async_copy(result_in.at[others], result_in.at[others], result_send).wait()


def finish_kernel(
    left_stats,
    right_stats,
    left_prod,
    right_prod,
    tiles,
    left_out,
    right_out,
    update,
    left_v,
    right_v,
    left_prod_v,
    right_prod_v,
    tiles_v,
    load_sem,
):
    col_blocks, share = update.shape[2:]
    sources = (tiles, left_stats, left_prod, right_stats, right_prod)
    targets = (tiles_v, left_v, left_prod_v, right_v, right_prod_v)
    copies = [
        pltpu.make_async_copy(source, target, load_sem.at[i])
        for i, (source, target) in enumerate(zip(sources, targets))
    ]
    for copy in copies:
        copy.start()
    copies[0].wait()
    for j in range(col_blocks):
        update[:, :, j, :] = tiles_v[:, :, j * share : (j + 1) * share]
    copies[1].wait()
    copies[2].wait()
    left_out[...] = decay_rate * left_v[...] + (1.0 - decay_rate) * left_prod_v[...]
    copies[3].wait()
    copies[4].wait()
    right_out[...] = decay_rate * right_v[...] + (1.0 - decay_rate) * right_prod_v[...]


def on_device(acts, dout, left_stats, right_stats, left_root, right_root, owner_of, counters):
    replicas, owners = lax.axis_size("dp"), lax.axis_size("owner")
    tokens, features = acts.shape
    col_blocks, share = dout.shape[1:]
    slots, rows, order = left_stats.shape
    row_blocks = features // order
    chips = replicas // 2
    half = chips // 2
    f32, bf16 = jnp.float32, jnp.bfloat16
    total = counters.shape[0]
    dout_rows = dout.transpose(1, 2, 0).reshape(col_blocks * share, tokens)
    vmem = functools.partial(pl.BlockSpec, memory_space=pltpu.VMEM)
    anywhere = functools.partial(pl.BlockSpec, memory_space=pl.ANY)
    kept = slots // 2
    ring_shape = (2, RING_GROUPS, half + 1, row_blocks // RING_GROUPS, rows, LANES)
    dma = pltpu.SemaphoreType.DMA
    left_prod, right_prod, update = pl.pallas_call(
        step_kernel,
        out_shape=(
            jax.ShapeDtypeStruct((slots, rows, order), f32),
            jax.ShapeDtypeStruct((slots, rows, order), f32),
            jax.ShapeDtypeStruct((row_blocks, rows, LANES), bf16),
        ),
        in_specs=[anywhere()] * 6,
        out_specs=(vmem(), vmem(), vmem()),
        scratch_shapes=[
            pltpu.VMEM((1, total), jnp.int32),
            pltpu.VMEM((1, total), jnp.int32),
            pltpu.VMEM((8, LANES), jnp.int32),
            pltpu.SMEM((8, LANES), jnp.int32),
            pltpu.VMEM((row_blocks, tokens, order), bf16),
            pltpu.VMEM((LANES, tokens), bf16),
            pltpu.VMEM((slots, rows, order), bf16),
            pltpu.VMEM((2, kept, rows, order), bf16),
            pltpu.VMEM((kept, order, order), bf16),
            pltpu.VMEM((row_blocks, chips, 2, rows, LANES), bf16),
            pltpu.VMEM((row_blocks, chips, rows, LANES), bf16),
            pltpu.VMEM(ring_shape, bf16),
            pltpu.VMEM(ring_shape, bf16),
            pltpu.VMEM((row_blocks * col_blocks + 1, rows, LANES), f32),
            pltpu.VMEM((owners, rows, LANES), bf16),
            pltpu.VMEM((owners, rows, LANES), bf16),
            pltpu.VMEM((slots, rows, order), bf16),
            pltpu.VMEM((replicas, kept, rows, order), bf16),
            pltpu.VMEM((kept, LANES // (2 * rows), 2 * rows, order), bf16),
            pltpu.VMEM((2, kept, rows, order), bf16),
            pltpu.VMEM((slots, rows, order), bf16),
            pltpu.VMEM((2, 2, kept, rows, order), f32),
            pltpu.VMEM((2, kept, rows, order), f32),
            pltpu.VMEM((1, LANES), f32),
            pltpu.VMEM((replicas, 1, LANES), f32),
            pltpu.VMEM((owners, rows, LANES), f32),
            pltpu.VMEM((owners, rows, LANES), f32),
            pltpu.VMEM((owners, rows, LANES), bf16),
            pltpu.VMEM((owners, rows, LANES), bf16),
            pltpu.VMEM((owners * col_blocks, rows, LANES), f32),
            dma((row_blocks,)),
            dma((6,)),
            dma((row_blocks,)),
            dma((row_blocks,)),
            dma((2, RING_GROUPS, half + 1)),
            dma((2, RING_GROUPS, half + 1)),
            dma,
            dma,
            dma((2, half)),
            dma((2, half)),
            dma((4,)),
            dma((4,)),
            dma,
            dma,
            dma,
            dma,
        ],
        compiler_params=pltpu.CompilerParams(
            collective_id=0, has_side_effects=True, vmem_limit_bytes=56 * 1024 * 1024
        ),
    )(owner_of.reshape(1, total), counters.reshape(1, total), dout_rows, acts, left_root, right_root)
    return pl.pallas_call(
        finish_kernel,
        out_shape=(
            jax.ShapeDtypeStruct((slots, rows, order), f32),
            jax.ShapeDtypeStruct((slots, rows, order), f32),
            jax.ShapeDtypeStruct((row_blocks, rows, col_blocks, share), bf16),
        ),
        in_specs=[anywhere()] * 5,
        out_specs=(vmem(), vmem(), vmem()),
        scratch_shapes=[pltpu.VMEM((slots, rows, order), f32)] * 4
        + [pltpu.VMEM((row_blocks, rows, LANES), bf16), dma((5,))],
    )(left_stats, right_stats, left_prod, right_prod, update)


def solution(mesh):
    in_specs = (
        P("dp", None),
        P("dp", None, "owner"),
        P("owner", "dp", None),
        P("owner", "dp", None),
        P("owner", "dp", None),
        P("owner", None, None),
        P(),
        P(),
    )
    out_specs = (P("owner", "dp", None), P("owner", "dp", None), P(None, "dp", None, "owner"))
    return jax.shard_map(
        on_device, mesh=mesh, in_specs=in_specs, out_specs=out_specs, check_vma=False
    )
```

```python
import functools

import jax
import jax.numpy as jnp
from jax import lax
from jax.experimental import pallas as pl
from jax.experimental.pallas import tpu as pltpu
from jax.sharding import PartitionSpec as P

WARMUP = 25
MESH = pl.DeviceIdType.MESH
LANES = 128
RING_GROUPS = 2
STOP = {1: 0, 2: 1, 3: 0, 4: 3, 5: 3, 6: 0, 7: 6, 8: 6}

decay_rate = 0.95
epsilon = 1e-06


def around(place, size):
    place = jnp.where(place >= size, place - size, place)
    return jnp.where(place < 0, place + size, place)


def far_first(size):
    return [(size // 2 + ((k + 1) // 2 if k % 2 else -(k // 2))) % size for k in range(size)]


def swing(size, visit):
    def step(k, carry):
        distance, stride, side = carry
        visit(distance)
        return distance + side * stride, stride + 1, -side

    lax.fori_loop(0, size - 1, step, (jnp.int32(size // 2), jnp.int32(1), jnp.int32(1)))


def place_tables(owner_row, counter_row, slot_count, col_blocks):
    total = owner_row.shape[1]
    square = (total, total)
    down = lax.broadcasted_iota(jnp.int32, square, 0)
    across = lax.broadcasted_iota(jnp.int32, square, 1)

    def upright(row):
        return jnp.sum(jnp.where(down == across, row, 0), axis=1, keepdims=True)

    owner_col, counter_col = upright(owner_row), upright(counter_row)
    same = owner_col == owner_row
    slot_col = jnp.sum(jnp.where(same & (across < down), 1, 0), axis=1, keepdims=True)
    slot_row = jnp.sum(jnp.where(same & (down < across), 1, 0), axis=0, keepdims=True)
    block_col, block_row = down[:, :1], across[:1, :]
    last = col_blocks - 1
    taken = (block_col & ~last) + ((slot_col - block_col) & last)
    given = owner_row * col_blocks + ((block_row - slot_row) & last)
    places = lax.broadcasted_iota(jnp.int32, (total, LANES), 1)
    hit = owner_col * slot_count + slot_col == places
    source = total + jnp.sum(jnp.where(hit, taken - total, 0), axis=0, keepdims=True)
    begun = jnp.sum(jnp.where(hit & (counter_col >= WARMUP), 1, 0), axis=0, keepdims=True)
    return source, given, begun


def step_kernel(
    owner_hbm,
    counter_hbm,
    dout_hbm,
    acts_hbm,
    left_root_hbm,
    right_root_hbm,
    left_prod,
    right_prod,
    update,
    owner_v,
    counter_v,
    table_v,
    table,
    acts_v,
    dout_v,
    left_root,
    roots,
    right_root,
    terms,
    sibling_terms,
    sum_out,
    sum_in,
    turned,
    tile_out,
    tile_in,
    own_grad,
    grads,
    flipped,
    pre_out,
    precond,
    prod_out,
    prod_in,
    norm_out,
    norm_in,
    pre_tiles,
    grad_tiles,
    result_out,
    result_in,
    returned,
    acts_sem,
    load_sem,
    pair_send,
    pair_recv,
    ring_send,
    ring_recv,
    tile_send,
    tile_recv,
    gather_send,
    gather_recv,
    swap_send,
    swap_recv,
    norm_send,
    norm_recv,
    result_send,
    result_recv,
):
    replica = lax.axis_index("dp")
    owner = lax.axis_index("owner")
    replicas = grads.shape[0]
    owners = tile_in.shape[0]
    chips = replicas // 2
    half = chips // 2
    chip = replica // 2
    core = lax.rem(replica, 2)
    row_blocks, tokens, order = acts_v.shape
    slots, rows, _ = own_grad.shape
    col_blocks = turned.shape[0] // row_blocks
    share = LANES // col_blocks
    group_rows = row_blocks // RING_GROUPS
    kept = slots // 2
    mine = pl.ds(core * kept, kept)
    theirs = pl.ds((1 - core) * kept, kept)
    f32, bf16 = jnp.float32, jnp.bfloat16

    def acts_copy(i):
        return pltpu.make_async_copy(
            acts_hbm.at[:, pl.ds(pl.multiple_of(i * order, order), order)],
            acts_v.at[i],
            acts_sem.at[i],
        )

    dout_copy = pltpu.make_async_copy(dout_hbm, dout_v, load_sem.at[0])
    left_copy = pltpu.make_async_copy(left_root_hbm, left_root, load_sem.at[1])
    right_copy = pltpu.make_async_copy(right_root_hbm.at[mine], right_root, load_sem.at[2])
    owner_copy = pltpu.make_async_copy(owner_hbm, owner_v, load_sem.at[3])
    counter_copy = pltpu.make_async_copy(counter_hbm, counter_v, load_sem.at[4])
    table_copy = pltpu.make_async_copy(table_v, table, load_sem.at[5])
    owner_copy.start()
    counter_copy.start()
    dout_copy.start()
    for i in range(row_blocks):
        acts_copy(i).start()
    left_copy.start()
    right_copy.start()

    across = min(4, owners)

    high, wide = owner // across, lax.rem(owner, across)
    beside = [around(wide + d, across) for d in far_first(across)]

    def each_owner(visit):
        def row(distance):
            y = around(high + distance, owners // across) * across
            for x in beside:
                visit(y + x)

        swing(owners // across, row)
        for x in beside[:-1]:
            visit(high * across + x)

    def each_replica(visit):
        def both(distance):
            there = around(chip + distance, chips) * 2
            visit(there)
            visit(there + 1)

        swing(chips, both)
        visit(chip * 2 + 1 - core)

    barrier = pltpu.get_barrier_semaphore()

    def greet_owner(peer):
        pl.semaphore_signal(barrier, inc=1, device_id=(replica, peer), device_id_type=MESH)

    def greet_replica(peer):
        pl.semaphore_signal(barrier, inc=1, device_id=(peer, owner), device_id_type=MESH)

    each_replica(greet_replica)
    each_owner(greet_owner)
    turned[row_blocks * col_blocks] = jnp.zeros((rows, LANES), f32)
    owner_copy.wait()
    counter_copy.wait()
    source, given, begun = place_tables(owner_v[...], counter_v[...], slots, col_blocks)
    table_v[0:1, :] = source
    table_v[1:2, 0 : row_blocks * col_blocks] = given
    table_v[2:3, :] = begun
    table_copy.start()
    dout_copy.wait()

    sibling = (chip * 2 + 1 - core, owner)
    up = (around(chip + 1, chips) * 2 + core, owner)
    down = (around(chip - 1, chips) * 2 + core, owner)

    def pair_copy(i):
        return pltpu.make_async_remote_copy(
            src_ref=terms.at[i, :, 1 - core],
            dst_ref=sibling_terms.at[i],
            send_sem=pair_send.at[i],
            recv_sem=pair_recv.at[i],
            device_id=sibling,
            device_id_type=MESH,
        )

    def term_step(i, carry):
        acts_copy(i).wait()
        part = jnp.dot(dout_v[...], acts_v[i], preferred_element_type=f32)
        terms[i] = part.T.astype(bf16).reshape(chips, 2, rows, LANES)
        return carry

    def term_and_pair(i, carry):
        term_step(i, carry)
        pair_copy(i).start()
        return carry

    early = row_blocks * 3 // 4
    lax.fori_loop(0, early, term_step, 0)
    pl.semaphore_wait(barrier, owners + replicas - 2)
    for i in range(early):
        pair_copy(i).start()
    lax.fori_loop(early, row_blocks, term_and_pair, 0)

    def swap_copy(which, source, target):
        return pltpu.make_async_remote_copy(
            src_ref=source,
            dst_ref=target,
            send_sem=swap_send.at[which],
            recv_sem=swap_recv.at[which],
            device_id=sibling,
            device_id_type=MESH,
        )

    root_swap = swap_copy(0, left_root.at[theirs], roots.at[core])
    grad_swap = swap_copy(1, own_grad.at[theirs], grads.at[replica])
    pre_swap = swap_copy(2, pre_out.at[1 - core], precond.at[mine])
    prod_swap = swap_copy(3, prod_out.at[1 - core], prod_in)
    left_copy.wait()
    root_swap.start()
    roots[core] = left_root[mine]

    def sum_copy(way, group, hops):
        step = hops - STOP[hops]
        peer = around(chip + (-step if way else step), chips) * 2 + core
        return pltpu.make_async_remote_copy(
            src_ref=sum_out.at[way, group, hops],
            dst_ref=sum_in.at[way, group, hops],
            send_sem=ring_send.at[way, group, hops],
            recv_sem=ring_recv.at[way, group, hops],
            device_id=(peer, owner),
            device_id_type=MESH,
        )

    def chip_terms(group, piece):
        here = pl.ds(group * group_rows, group_rows)
        return terms[here, piece, core].astype(f32) + sibling_terms[here, piece].astype(f32)

    def arrived(way, group, hops):
        sum_copy(way, group, hops).wait_recv()
        return sum_in[way, group, hops].astype(f32)

    def pass_on(way, group, hops):
        total = chip_terms(group, around(chip + (-hops if way else hops), chips))
        for other in routes[way]:
            if STOP[other] == hops:
                total = total + arrived(way, group, other)
        sum_out[way, group, hops] = total.astype(bf16)
        sum_copy(way, group, hops).start()

    routes = [range(1, half + 1), range(1, half)]
    for group in range(RING_GROUPS):
        for i in range(group * group_rows, (group + 1) * group_rows):
            pair_copy(i).wait_recv()
        for hops in range(half, 0, -1):
            for way in range(2):
                if hops in routes[way] and STOP[hops]:
                    pass_on(way, group, hops)
    for group in range(RING_GROUPS):
        for hops in range(half, 0, -1):
            for way in range(2):
                if hops in routes[way] and not STOP[hops]:
                    pass_on(way, group, hops)

    for group in range(RING_GROUPS):
        total = chip_terms(group, chip)
        for hops in range(1, half + 1):
            for way in range(2):
                if hops in routes[way] and not STOP[hops]:
                    total = total + arrived(way, group, hops)
        total = total.astype(bf16).astype(f32)
        for i in range(group_rows):
            for k in range(col_blocks):
                tile = total[i] if k == 0 else pltpu.roll(total[i], k * share, 1)
                turned[(group * group_rows + i) * col_blocks + k] = tile

    lane_block = lax.broadcasted_iota(jnp.int32, (rows, LANES), 1) // share

    table_copy.wait()

    def tile_copy(peer):
        return pltpu.make_async_remote_copy(
            src_ref=tile_out.at[peer],
            dst_ref=tile_in.at[owner],
            send_sem=tile_send,
            recv_sem=tile_recv,
            device_id=(replica, peer),
            device_id_type=MESH,
        )

    def tiles_for(peer):
        tile = jnp.zeros((rows, LANES), f32)
        for s in range(slots):
            tile = jnp.where(lane_block == s, turned[table[0, peer * slots + s]], tile)
        return tile.astype(bf16)

    def tile_step(peer):
        tile_out[peer] = tiles_for(peer)
        tile_copy(peer).start()

    each_owner(tile_step)
    tile_in[owner] = tiles_for(owner)
    others = pl.ds(0, owners - 1)
    pltpu.make_async_copy(tile_in.at[others], tile_in.at[others], tile_recv).wait()

    pieces = [tile_in[o].astype(f32) for o in range(owners)]
    for s in range(slots):
        for q in range(order // LANES):
            tile = jnp.zeros((rows, LANES), f32)
            for k in range(col_blocks):
                shift = (k - s) * share % LANES
                piece = pieces[q * col_blocks + k]
                piece = pltpu.roll(piece, shift, 1) if shift else piece
                tile = jnp.where(lane_block == k, piece, tile)
            own_grad[s, :, q * LANES : (q + 1) * LANES] = tile.astype(bf16)
    grad_swap.start()
    grads[replica] = own_grad[mine]

    def gather_copy(way, step):
        there = around(chip + (step if way else -step), chips)
        piece = grads.at[pl.ds(there * 2, 2)]
        return pltpu.make_async_remote_copy(
            src_ref=piece,
            dst_ref=piece,
            send_sem=gather_send.at[way, step],
            recv_sem=gather_recv.at[way, step],
            device_id=down if way else up,
            device_id_type=MESH,
        )

    grad_swap.wait_recv()
    gather_copy(0, 0).start()
    if half > 1:
        gather_copy(1, 0).start()

    lane = lax.broadcasted_iota(jnp.int32, (1, LANES), 1)
    norms = jnp.zeros((1, LANES), f32)
    for s in range(slots):
        own = own_grad[s].astype(f32)
        square = jnp.sum(own * own, axis=(0, 1), keepdims=True)
        norms = jnp.where(lane == slots + s, square, norms)

    def gather_round(step, carry):
        for way in range(2):
            gather_copy(way, step - 1).wait_recv()
            gather_copy(way, step).start()
        return carry

    lax.fori_loop(1, half - 1, gather_round, 0)
    if half > 1:
        gather_copy(0, half - 2).wait_recv()
        gather_copy(0, half - 1).start()
    root_swap.wait_recv()
    right_copy.wait()
    if half > 1:
        gather_copy(1, half - 2).wait_recv()
    gather_copy(0, half - 1).wait_recv()

    for t in range(kept):
        whole = grads[:, t].reshape(order, order)
        root = roots[:, t].reshape(2 * rows, order)
        inner = jnp.dot(root, whole, preferred_element_type=f32).astype(bf16)
        pre = jnp.dot(inner, right_root[t], preferred_element_type=f32).astype(bf16)
        pre_out[:, t] = pre.reshape(2, rows, order)
        pre = pre.astype(f32)
        square = jnp.sum(pre * pre, axis=(0, 1), keepdims=True)
        norms = jnp.where(lane == core * kept + t, square, norms)
    norm_out[...] = norms

    def norm_copy(peer):
        return pltpu.make_async_remote_copy(
            src_ref=norm_out,
            dst_ref=norm_in.at[replica],
            send_sem=norm_send,
            recv_sem=norm_recv,
            device_id=(peer, owner),
            device_id_type=MESH,
        )

    def norm_step(peer):
        norm_copy(peer).start()

    each_replica(norm_step)
    pre_swap.start()
    norm_in[replica] = norms
    precond[mine] = pre_out[core]

    span = pl.ds(pl.multiple_of(chip * 2 * rows // LANES * LANES, LANES), LANES)
    for t in range(kept):
        whole = grads[:, t].reshape(order, order)
        both = grads[pl.ds(chip * 2, 2), t].reshape(2 * rows, order)
        left = lax.dot_general(
            both, whole, (((1,), (1,)), ((), ())), preferred_element_type=f32
        )
        columns = grads[:, t, :, span].reshape(order, LANES)
        flipped[t] = columns.T.reshape(LANES // (2 * rows), 2 * rows, order)
        turned_rows = flipped[t, lax.rem(chip, LANES // (2 * rows))]
        right = jnp.dot(turned_rows, whole, preferred_element_type=f32)
        prod_out[:, 0, t] = left.reshape(2, rows, order)
        prod_out[:, 1, t] = right.reshape(2, rows, order)
    prod_swap.start()
    left_prod[mine] = prod_out[core, 0]
    right_prod[mine] = prod_out[core, 1]

    pre_swap.wait_recv()

    for q in range(order // LANES):
        here = slice(q * LANES, (q + 1) * LANES)
        pre_parts = [precond[s, :, here].astype(f32) for s in range(slots)]
        own_parts = [own_grad[s, :, here].astype(f32) for s in range(slots)]
        for k in range(col_blocks):
            pre_tile = jnp.zeros((rows, LANES), f32)
            own_tile = jnp.zeros((rows, LANES), f32)
            for s in range(slots):
                shift = (s - k) * share % LANES
                pre_part, own_part = pre_parts[s], own_parts[s]
                if shift:
                    pre_part = pltpu.roll(pre_part, shift, 1)
                    own_part = pltpu.roll(own_part, shift, 1)
                pre_tile = jnp.where(lane_block == s, pre_part, pre_tile)
                own_tile = jnp.where(lane_block == s, own_part, own_tile)
            pre_tiles[q * col_blocks + k] = pre_tile
            grad_tiles[q * col_blocks + k] = own_tile

    other_replicas = pl.ds(0, replicas - 1)
    pltpu.make_async_copy(
        norm_in.at[other_replicas], norm_in.at[other_replicas], norm_recv
    ).wait()
    norms = jnp.sum(norm_in[...], axis=0)
    scale = jnp.zeros((1, LANES), f32)
    started = jnp.zeros((1, LANES), jnp.int32)
    for s in range(slots):
        graft = jnp.sqrt(norms[:, slots + s : slots + s + 1] / (norms[:, s : s + 1] + epsilon))
        scale = jnp.where(lane // share == s, graft, scale)
        started = jnp.where(lane // share == s, table[2, owner * slots + s], started)

    def result_copy(peer):
        return pltpu.make_async_remote_copy(
            src_ref=result_out.at[peer],
            dst_ref=result_in.at[owner],
            send_sem=result_send,
            recv_sem=result_recv,
            device_id=(replica, peer),
            device_id_type=MESH,
        )

    def result_for(peer):
        return jnp.where(started > 0, pre_tiles[peer] * scale, grad_tiles[peer]).astype(bf16)

    def result_step(peer):
        result_out[peer] = result_for(peer)
        result_copy(peer).start()

    each_owner(result_step)
    result_in[owner] = result_for(owner)

    pltpu.make_async_copy(result_in.at[others], result_in.at[others], result_recv).wait()

    def turn_step(o, carry):
        tile = result_in[o].astype(f32)
        for k in range(col_blocks):
            returned[o * col_blocks + k] = pltpu.roll(tile, k * share, 1) if k else tile
        return carry

    lax.fori_loop(0, owners, turn_step, 0)

    def update_step(i, carry):
        tile = jnp.zeros((rows, LANES), f32)
        for j in range(col_blocks):
            tile = jnp.where(lane_block == j, returned[table[1, i * col_blocks + j]], tile)
        update[i] = tile.astype(bf16)
        return carry

    lax.fori_loop(0, row_blocks, update_step, 0)

    prod_swap.wait_recv()
    left_prod[theirs] = prod_in[0]
    right_prod[theirs] = prod_in[1]

    root_swap.wait_send()
    grad_swap.wait_send()
    pre_swap.wait_send()
    prod_swap.wait_send()
    for i in range(row_blocks):
        pair_copy(i).wait_send()

    def sent(step, carry):
        for way in range(2):
            gather_copy(way, step).wait_send()
        return carry

    lax.fori_loop(0, half - 1, sent, 0)
    for way in range(2):
        for group in range(RING_GROUPS):
            for hops in routes[way]:
                sum_copy(way, group, hops).wait_send()
    gather_copy(0, half - 1).wait_send()
    pltpu.make_async_copy(tile_in.at[others], tile_in.at[others], tile_send).wait()
    pltpu.make_async_copy(
        norm_in.at[other_replicas], norm_in.at[other_replicas], norm_send
    ).wait()
    pltpu.make_async_copy(result_in.at[others], result_in.at[others], result_send).wait()


def finish_kernel(
    left_stats,
    right_stats,
    left_prod,
    right_prod,
    tiles,
    left_out,
    right_out,
    update,
    left_v,
    right_v,
    left_prod_v,
    right_prod_v,
    tiles_v,
    load_sem,
):
    col_blocks, share = update.shape[2:]
    sources = (tiles, left_stats, left_prod, right_stats, right_prod)
    targets = (tiles_v, left_v, left_prod_v, right_v, right_prod_v)
    copies = [
        pltpu.make_async_copy(source, target, load_sem.at[i])
        for i, (source, target) in enumerate(zip(sources, targets))
    ]
    for copy in copies:
        copy.start()
    copies[0].wait()
    for j in range(col_blocks):
        update[:, :, j, :] = tiles_v[:, :, j * share : (j + 1) * share]
    copies[1].wait()
    copies[2].wait()
    left_out[...] = decay_rate * left_v[...] + (1.0 - decay_rate) * left_prod_v[...]
    copies[3].wait()
    copies[4].wait()
    right_out[...] = decay_rate * right_v[...] + (1.0 - decay_rate) * right_prod_v[...]


def on_device(acts, dout, left_stats, right_stats, left_root, right_root, owner_of, counters):
    replicas, owners = lax.axis_size("dp"), lax.axis_size("owner")
    tokens, features = acts.shape
    col_blocks, share = dout.shape[1:]
    slots, rows, order = left_stats.shape
    row_blocks = features // order
    chips = replicas // 2
    half = chips // 2
    f32, bf16 = jnp.float32, jnp.bfloat16
    total = counters.shape[0]
    dout_rows = dout.transpose(1, 2, 0).reshape(col_blocks * share, tokens)
    vmem = functools.partial(pl.BlockSpec, memory_space=pltpu.VMEM)
    anywhere = functools.partial(pl.BlockSpec, memory_space=pl.ANY)
    kept = slots // 2
    ring_shape = (2, RING_GROUPS, half + 1, row_blocks // RING_GROUPS, rows, LANES)
    dma = pltpu.SemaphoreType.DMA
    left_prod, right_prod, update = pl.pallas_call(
        step_kernel,
        out_shape=(
            jax.ShapeDtypeStruct((slots, rows, order), f32),
            jax.ShapeDtypeStruct((slots, rows, order), f32),
            jax.ShapeDtypeStruct((row_blocks, rows, LANES), bf16),
        ),
        in_specs=[anywhere()] * 6,
        out_specs=(vmem(), vmem(), vmem()),
        scratch_shapes=[
            pltpu.VMEM((1, total), jnp.int32),
            pltpu.VMEM((1, total), jnp.int32),
            pltpu.VMEM((8, LANES), jnp.int32),
            pltpu.SMEM((8, LANES), jnp.int32),
            pltpu.VMEM((row_blocks, tokens, order), bf16),
            pltpu.VMEM((LANES, tokens), bf16),
            pltpu.VMEM((slots, rows, order), bf16),
            pltpu.VMEM((2, kept, rows, order), bf16),
            pltpu.VMEM((kept, order, order), bf16),
            pltpu.VMEM((row_blocks, chips, 2, rows, LANES), bf16),
            pltpu.VMEM((row_blocks, chips, rows, LANES), bf16),
            pltpu.VMEM(ring_shape, bf16),
            pltpu.VMEM(ring_shape, bf16),
            pltpu.VMEM((row_blocks * col_blocks + 1, rows, LANES), f32),
            pltpu.VMEM((owners, rows, LANES), bf16),
            pltpu.VMEM((owners, rows, LANES), bf16),
            pltpu.VMEM((slots, rows, order), bf16),
            pltpu.VMEM((replicas, kept, rows, order), bf16),
            pltpu.VMEM((kept, LANES // (2 * rows), 2 * rows, order), bf16),
            pltpu.VMEM((2, kept, rows, order), bf16),
            pltpu.VMEM((slots, rows, order), bf16),
            pltpu.VMEM((2, 2, kept, rows, order), f32),
            pltpu.VMEM((2, kept, rows, order), f32),
            pltpu.VMEM((1, LANES), f32),
            pltpu.VMEM((replicas, 1, LANES), f32),
            pltpu.VMEM((owners, rows, LANES), f32),
            pltpu.VMEM((owners, rows, LANES), f32),
            pltpu.VMEM((owners, rows, LANES), bf16),
            pltpu.VMEM((owners, rows, LANES), bf16),
            pltpu.VMEM((owners * col_blocks, rows, LANES), f32),
            dma((row_blocks,)),
            dma((6,)),
            dma((row_blocks,)),
            dma((row_blocks,)),
            dma((2, RING_GROUPS, half + 1)),
            dma((2, RING_GROUPS, half + 1)),
            dma,
            dma,
            dma((2, half)),
            dma((2, half)),
            dma((4,)),
            dma((4,)),
            dma,
            dma,
            dma,
            dma,
        ],
        compiler_params=pltpu.CompilerParams(
            collective_id=0, has_side_effects=True, vmem_limit_bytes=56 * 1024 * 1024
        ),
    )(owner_of.reshape(1, total), counters.reshape(1, total), dout_rows, acts, left_root, right_root)
    return pl.pallas_call(
        finish_kernel,
        out_shape=(
            jax.ShapeDtypeStruct((slots, rows, order), f32),
            jax.ShapeDtypeStruct((slots, rows, order), f32),
            jax.ShapeDtypeStruct((row_blocks, rows, col_blocks, share), bf16),
        ),
        in_specs=[anywhere()] * 5,
        out_specs=(vmem(), vmem(), vmem()),
        scratch_shapes=[pltpu.VMEM((slots, rows, order), f32)] * 4
        + [pltpu.VMEM((row_blocks, rows, LANES), bf16), dma((5,))],
    )(left_stats, right_stats, left_prod, right_prod, update)


def solution(mesh):
    in_specs = (
        P("dp", None),
        P("dp", None, "owner"),
        P("owner", "dp", None),
        P("owner", "dp", None),
        P("owner", "dp", None),
        P("owner", None, None),
        P(),
        P(),
    )
    out_specs = (P("owner", "dp", None), P("owner", "dp", None), P(None, "dp", None, "owner"))
    return jax.shard_map(
        on_device, mesh=mesh, in_specs=in_specs, out_specs=out_specs, check_vma=False
    )
```

```python
import functools

import jax
import jax.numpy as jnp
from jax import lax
from jax.experimental import pallas as pl
from jax.experimental.pallas import tpu as pltpu
from jax.sharding import PartitionSpec as P

WARMUP = 25
MESH = pl.DeviceIdType.MESH
LANES = 128
RING_GROUPS = 2
STOP = {1: 0, 2: 0, 3: 2, 4: 2, 5: 0, 6: 5, 7: 5, 8: 5}

decay_rate = 0.95
epsilon = 1e-06


def around(place, size):
    place = jnp.where(place >= size, place - size, place)
    return jnp.where(place < 0, place + size, place)


def far_first(size):
    return [(size // 2 + ((k + 1) // 2 if k % 2 else -(k // 2))) % size for k in range(size)]


def swing(size, visit):
    def step(k, carry):
        distance, stride, side = carry
        visit(distance)
        return distance + side * stride, stride + 1, -side

    lax.fori_loop(0, size - 1, step, (jnp.int32(size // 2), jnp.int32(1), jnp.int32(1)))


def place_tables(owner_row, counter_row, slot_count, col_blocks):
    total = owner_row.shape[1]
    square = (total, total)
    down = lax.broadcasted_iota(jnp.int32, square, 0)
    across = lax.broadcasted_iota(jnp.int32, square, 1)

    def upright(row):
        return jnp.sum(jnp.where(down == across, row, 0), axis=1, keepdims=True)

    owner_col, counter_col = upright(owner_row), upright(counter_row)
    same = owner_col == owner_row
    slot_col = jnp.sum(jnp.where(same & (across < down), 1, 0), axis=1, keepdims=True)
    slot_row = jnp.sum(jnp.where(same & (down < across), 1, 0), axis=0, keepdims=True)
    block_col, block_row = down[:, :1], across[:1, :]
    last = col_blocks - 1
    taken = (block_col & ~last) + ((slot_col - block_col) & last)
    given = owner_row * col_blocks + ((block_row - slot_row) & last)
    places = lax.broadcasted_iota(jnp.int32, (total, LANES), 1)
    hit = owner_col * slot_count + slot_col == places
    source = total + jnp.sum(jnp.where(hit, taken - total, 0), axis=0, keepdims=True)
    begun = jnp.sum(jnp.where(hit & (counter_col >= WARMUP), 1, 0), axis=0, keepdims=True)
    return source, given, begun


def step_kernel(
    owner_hbm,
    counter_hbm,
    dout_hbm,
    acts_hbm,
    left_root_hbm,
    right_root_hbm,
    left_prod,
    right_prod,
    update,
    owner_v,
    counter_v,
    table_v,
    table,
    acts_v,
    dout_v,
    left_root,
    roots,
    right_root,
    terms,
    sibling_terms,
    sum_out,
    sum_in,
    turned,
    tile_out,
    tile_in,
    own_grad,
    grads,
    flipped,
    pre_out,
    precond,
    prod_out,
    prod_in,
    norm_out,
    norm_in,
    pre_tiles,
    grad_tiles,
    result_out,
    result_in,
    returned,
    acts_sem,
    load_sem,
    pair_send,
    pair_recv,
    ring_send,
    ring_recv,
    tile_send,
    tile_recv,
    gather_send,
    gather_recv,
    swap_send,
    swap_recv,
    norm_send,
    norm_recv,
    result_send,
    result_recv,
):
    replica = lax.axis_index("dp")
    owner = lax.axis_index("owner")
    replicas = grads.shape[0]
    owners = tile_in.shape[0]
    chips = replicas // 2
    half = chips // 2
    chip = replica // 2
    core = lax.rem(replica, 2)
    row_blocks, tokens, order = acts_v.shape
    slots, rows, _ = own_grad.shape
    col_blocks = turned.shape[0] // row_blocks
    share = LANES // col_blocks
    group_rows = row_blocks // RING_GROUPS
    kept = slots // 2
    mine = pl.ds(core * kept, kept)
    theirs = pl.ds((1 - core) * kept, kept)
    f32, bf16 = jnp.float32, jnp.bfloat16

    def acts_copy(i):
        return pltpu.make_async_copy(
            acts_hbm.at[:, pl.ds(pl.multiple_of(i * order, order), order)],
            acts_v.at[i],
            acts_sem.at[i],
        )

    dout_copy = pltpu.make_async_copy(dout_hbm, dout_v, load_sem.at[0])
    left_copy = pltpu.make_async_copy(left_root_hbm, left_root, load_sem.at[1])
    right_copy = pltpu.make_async_copy(right_root_hbm.at[mine], right_root, load_sem.at[2])
    owner_copy = pltpu.make_async_copy(owner_hbm, owner_v, load_sem.at[3])
    counter_copy = pltpu.make_async_copy(counter_hbm, counter_v, load_sem.at[4])
    table_copy = pltpu.make_async_copy(table_v, table, load_sem.at[5])
    owner_copy.start()
    counter_copy.start()
    dout_copy.start()
    for i in range(row_blocks):
        acts_copy(i).start()
    left_copy.start()
    right_copy.start()

    across = min(4, owners)

    high, wide = owner // across, lax.rem(owner, across)
    beside = [around(wide + d, across) for d in far_first(across)]

    def each_owner(visit):
        def row(distance):
            y = around(high + distance, owners // across) * across
            for x in beside:
                visit(y + x)

        swing(owners // across, row)
        for x in beside[:-1]:
            visit(high * across + x)

    def each_replica(visit):
        def both(distance):
            there = around(chip + distance, chips) * 2
            visit(there)
            visit(there + 1)

        swing(chips, both)
        visit(chip * 2 + 1 - core)

    barrier = pltpu.get_barrier_semaphore()

    def greet_owner(peer):
        pl.semaphore_signal(barrier, inc=1, device_id=(replica, peer), device_id_type=MESH)

    def greet_replica(peer):
        pl.semaphore_signal(barrier, inc=1, device_id=(peer, owner), device_id_type=MESH)

    each_replica(greet_replica)
    each_owner(greet_owner)
    turned[row_blocks * col_blocks] = jnp.zeros((rows, LANES), f32)
    owner_copy.wait()
    counter_copy.wait()
    source, given, begun = place_tables(owner_v[...], counter_v[...], slots, col_blocks)
    table_v[0:1, :] = source
    table_v[1:2, 0 : row_blocks * col_blocks] = given
    table_v[2:3, :] = begun
    table_copy.start()
    dout_copy.wait()

    sibling = (chip * 2 + 1 - core, owner)
    up = (around(chip + 1, chips) * 2 + core, owner)
    down = (around(chip - 1, chips) * 2 + core, owner)

    def pair_copy(i):
        return pltpu.make_async_remote_copy(
            src_ref=terms.at[i, :, 1 - core],
            dst_ref=sibling_terms.at[i],
            send_sem=pair_send.at[i],
            recv_sem=pair_recv.at[i],
            device_id=sibling,
            device_id_type=MESH,
        )

    def term_step(i, carry):
        acts_copy(i).wait()
        part = jnp.dot(dout_v[...], acts_v[i], preferred_element_type=f32)
        terms[i] = part.T.astype(bf16).reshape(chips, 2, rows, LANES)
        return carry

    def term_and_pair(i, carry):
        term_step(i, carry)
        pair_copy(i).start()
        return carry

    early = row_blocks * 3 // 4
    lax.fori_loop(0, early, term_step, 0)
    pl.semaphore_wait(barrier, owners + replicas - 2)
    for i in range(early):
        pair_copy(i).start()
    lax.fori_loop(early, row_blocks, term_and_pair, 0)

    def swap_copy(which, source, target):
        return pltpu.make_async_remote_copy(
            src_ref=source,
            dst_ref=target,
            send_sem=swap_send.at[which],
            recv_sem=swap_recv.at[which],
            device_id=sibling,
            device_id_type=MESH,
        )

    root_swap = swap_copy(0, left_root.at[theirs], roots.at[core])
    grad_swap = swap_copy(1, own_grad.at[theirs], grads.at[replica])
    pre_swap = swap_copy(2, pre_out.at[1 - core], precond.at[mine])
    prod_swap = swap_copy(3, prod_out.at[1 - core], prod_in)
    left_copy.wait()
    root_swap.start()
    roots[core] = left_root[mine]

    def sum_copy(way, group, hops):
        step = hops - STOP[hops]
        peer = around(chip + (-step if way else step), chips) * 2 + core
        return pltpu.make_async_remote_copy(
            src_ref=sum_out.at[way, group, hops],
            dst_ref=sum_in.at[way, group, hops],
            send_sem=ring_send.at[way, group, hops],
            recv_sem=ring_recv.at[way, group, hops],
            device_id=(peer, owner),
            device_id_type=MESH,
        )

    def chip_terms(group, piece):
        here = pl.ds(group * group_rows, group_rows)
        return terms[here, piece, core].astype(f32) + sibling_terms[here, piece].astype(f32)

    def arrived(way, group, hops):
        sum_copy(way, group, hops).wait_recv()
        return sum_in[way, group, hops].astype(f32)

    def pass_on(way, group, hops):
        total = chip_terms(group, around(chip + (-hops if way else hops), chips))
        for other in routes[way]:
            if STOP[other] == hops:
                total = total + arrived(way, group, other)
        sum_out[way, group, hops] = total.astype(bf16)
        sum_copy(way, group, hops).start()

    routes = [range(1, half + 1), range(1, half)]
    for group in range(RING_GROUPS):
        for i in range(group * group_rows, (group + 1) * group_rows):
            pair_copy(i).wait_recv()
        for hops in range(half, 0, -1):
            for way in range(2):
                if hops in routes[way] and STOP[hops]:
                    pass_on(way, group, hops)
    for group in range(RING_GROUPS):
        for hops in range(half, 0, -1):
            for way in range(2):
                if hops in routes[way] and not STOP[hops]:
                    pass_on(way, group, hops)

    for group in range(RING_GROUPS):
        total = chip_terms(group, chip)
        for hops in range(1, half + 1):
            for way in range(2):
                if hops in routes[way] and not STOP[hops]:
                    total = total + arrived(way, group, hops)
        total = total.astype(bf16).astype(f32)
        for i in range(group_rows):
            for k in range(col_blocks):
                tile = total[i] if k == 0 else pltpu.roll(total[i], k * share, 1)
                turned[(group * group_rows + i) * col_blocks + k] = tile

    lane_block = lax.broadcasted_iota(jnp.int32, (rows, LANES), 1) // share

    table_copy.wait()

    def tile_copy(peer):
        return pltpu.make_async_remote_copy(
            src_ref=tile_out.at[peer],
            dst_ref=tile_in.at[owner],
            send_sem=tile_send,
            recv_sem=tile_recv,
            device_id=(replica, peer),
            device_id_type=MESH,
        )

    def tiles_for(peer):
        tile = jnp.zeros((rows, LANES), f32)
        for s in range(slots):
            tile = jnp.where(lane_block == s, turned[table[0, peer * slots + s]], tile)
        return tile.astype(bf16)

    def tile_step(peer):
        tile_out[peer] = tiles_for(peer)
        tile_copy(peer).start()

    each_owner(tile_step)
    tile_in[owner] = tiles_for(owner)
    others = pl.ds(0, owners - 1)
    pltpu.make_async_copy(tile_in.at[others], tile_in.at[others], tile_recv).wait()

    pieces = [tile_in[o].astype(f32) for o in range(owners)]
    for s in range(slots):
        for q in range(order // LANES):
            tile = jnp.zeros((rows, LANES), f32)
            for k in range(col_blocks):
                shift = (k - s) * share % LANES
                piece = pieces[q * col_blocks + k]
                piece = pltpu.roll(piece, shift, 1) if shift else piece
                tile = jnp.where(lane_block == k, piece, tile)
            own_grad[s, :, q * LANES : (q + 1) * LANES] = tile.astype(bf16)
    grad_swap.start()
    grads[replica] = own_grad[mine]

    def gather_copy(way, step):
        there = around(chip + (step if way else -step), chips)
        piece = grads.at[pl.ds(there * 2, 2)]
        return pltpu.make_async_remote_copy(
            src_ref=piece,
            dst_ref=piece,
            send_sem=gather_send.at[way, step],
            recv_sem=gather_recv.at[way, step],
            device_id=down if way else up,
            device_id_type=MESH,
        )

    grad_swap.wait_recv()
    gather_copy(0, 0).start()
    if half > 1:
        gather_copy(1, 0).start()

    lane = lax.broadcasted_iota(jnp.int32, (1, LANES), 1)
    norms = jnp.zeros((1, LANES), f32)
    for s in range(slots):
        own = own_grad[s].astype(f32)
        square = jnp.sum(own * own, axis=(0, 1), keepdims=True)
        norms = jnp.where(lane == slots + s, square, norms)

    def gather_round(step, carry):
        for way in range(2):
            gather_copy(way, step - 1).wait_recv()
            gather_copy(way, step).start()
        return carry

    lax.fori_loop(1, half - 1, gather_round, 0)
    if half > 1:
        gather_copy(0, half - 2).wait_recv()
        gather_copy(0, half - 1).start()
    root_swap.wait_recv()
    right_copy.wait()
    if half > 1:
        gather_copy(1, half - 2).wait_recv()
    gather_copy(0, half - 1).wait_recv()

    for t in range(kept):
        whole = grads[:, t].reshape(order, order)
        root = roots[:, t].reshape(2 * rows, order)
        inner = jnp.dot(root, whole, preferred_element_type=f32).astype(bf16)
        pre = jnp.dot(inner, right_root[t], preferred_element_type=f32).astype(bf16)
        pre_out[:, t] = pre.reshape(2, rows, order)
        pre = pre.astype(f32)
        square = jnp.sum(pre * pre, axis=(0, 1), keepdims=True)
        norms = jnp.where(lane == core * kept + t, square, norms)
    norm_out[...] = norms

    def norm_copy(peer):
        return pltpu.make_async_remote_copy(
            src_ref=norm_out,
            dst_ref=norm_in.at[replica],
            send_sem=norm_send,
            recv_sem=norm_recv,
            device_id=(peer, owner),
            device_id_type=MESH,
        )

    def norm_step(peer):
        norm_copy(peer).start()

    each_replica(norm_step)
    pre_swap.start()
    norm_in[replica] = norms
    precond[mine] = pre_out[core]

    span = pl.ds(pl.multiple_of(chip * 2 * rows // LANES * LANES, LANES), LANES)
    for t in range(kept):
        whole = grads[:, t].reshape(order, order)
        both = grads[pl.ds(chip * 2, 2), t].reshape(2 * rows, order)
        left = lax.dot_general(
            both, whole, (((1,), (1,)), ((), ())), preferred_element_type=f32
        )
        columns = grads[:, t, :, span].reshape(order, LANES)
        flipped[t] = columns.T.reshape(LANES // (2 * rows), 2 * rows, order)
        turned_rows = flipped[t, lax.rem(chip, LANES // (2 * rows))]
        right = jnp.dot(turned_rows, whole, preferred_element_type=f32)
        prod_out[:, 0, t] = left.reshape(2, rows, order)
        prod_out[:, 1, t] = right.reshape(2, rows, order)
    prod_swap.start()
    left_prod[mine] = prod_out[core, 0]
    right_prod[mine] = prod_out[core, 1]

    pre_swap.wait_recv()

    for q in range(order // LANES):
        here = slice(q * LANES, (q + 1) * LANES)
        pre_parts = [precond[s, :, here].astype(f32) for s in range(slots)]
        own_parts = [own_grad[s, :, here].astype(f32) for s in range(slots)]
        for k in range(col_blocks):
            pre_tile = jnp.zeros((rows, LANES), f32)
            own_tile = jnp.zeros((rows, LANES), f32)
            for s in range(slots):
                shift = (s - k) * share % LANES
                pre_part, own_part = pre_parts[s], own_parts[s]
                if shift:
                    pre_part = pltpu.roll(pre_part, shift, 1)
                    own_part = pltpu.roll(own_part, shift, 1)
                pre_tile = jnp.where(lane_block == s, pre_part, pre_tile)
                own_tile = jnp.where(lane_block == s, own_part, own_tile)
            pre_tiles[q * col_blocks + k] = pre_tile
            grad_tiles[q * col_blocks + k] = own_tile

    other_replicas = pl.ds(0, replicas - 1)
    pltpu.make_async_copy(
        norm_in.at[other_replicas], norm_in.at[other_replicas], norm_recv
    ).wait()
    norms = jnp.sum(norm_in[...], axis=0)
    scale = jnp.zeros((1, LANES), f32)
    started = jnp.zeros((1, LANES), jnp.int32)
    for s in range(slots):
        graft = jnp.sqrt(norms[:, slots + s : slots + s + 1] / (norms[:, s : s + 1] + epsilon))
        scale = jnp.where(lane // share == s, graft, scale)
        started = jnp.where(lane // share == s, table[2, owner * slots + s], started)

    def result_copy(peer):
        return pltpu.make_async_remote_copy(
            src_ref=result_out.at[peer],
            dst_ref=result_in.at[owner],
            send_sem=result_send,
            recv_sem=result_recv,
            device_id=(replica, peer),
            device_id_type=MESH,
        )

    def result_for(peer):
        return jnp.where(started > 0, pre_tiles[peer] * scale, grad_tiles[peer]).astype(bf16)

    def result_step(peer):
        result_out[peer] = result_for(peer)
        result_copy(peer).start()

    each_owner(result_step)
    result_in[owner] = result_for(owner)

    pltpu.make_async_copy(result_in.at[others], result_in.at[others], result_recv).wait()

    batch = min(8, owners)

    def turn_step(n, carry):
        for o in range(batch):
            tile = result_in[n * batch + o].astype(f32)
            for k in range(col_blocks):
                place = (n * batch + o) * col_blocks + k
                returned[place] = pltpu.roll(tile, k * share, 1) if k else tile
        return carry

    lax.fori_loop(0, owners // batch, turn_step, 0)

    def update_step(i, carry):
        tile = jnp.zeros((rows, LANES), f32)
        for j in range(col_blocks):
            tile = jnp.where(lane_block == j, returned[table[1, i * col_blocks + j]], tile)
        update[i] = tile.astype(bf16)
        return carry

    lax.fori_loop(0, row_blocks, update_step, 0)

    prod_swap.wait_recv()
    left_prod[theirs] = prod_in[0]
    right_prod[theirs] = prod_in[1]

    root_swap.wait_send()
    grad_swap.wait_send()
    pre_swap.wait_send()
    prod_swap.wait_send()
    for i in range(row_blocks):
        pair_copy(i).wait_send()

    def sent(step, carry):
        for way in range(2):
            gather_copy(way, step).wait_send()
        return carry

    lax.fori_loop(0, half - 1, sent, 0)
    for way in range(2):
        for group in range(RING_GROUPS):
            for hops in routes[way]:
                sum_copy(way, group, hops).wait_send()
    gather_copy(0, half - 1).wait_send()
    pltpu.make_async_copy(tile_in.at[others], tile_in.at[others], tile_send).wait()
    pltpu.make_async_copy(
        norm_in.at[other_replicas], norm_in.at[other_replicas], norm_send
    ).wait()
    pltpu.make_async_copy(result_in.at[others], result_in.at[others], result_send).wait()


def finish_kernel(
    left_stats,
    right_stats,
    left_prod,
    right_prod,
    tiles,
    left_out,
    right_out,
    update,
    left_v,
    right_v,
    left_prod_v,
    right_prod_v,
    tiles_v,
    load_sem,
):
    col_blocks, share = update.shape[2:]
    sources = (tiles, left_stats, left_prod, right_stats, right_prod)
    targets = (tiles_v, left_v, left_prod_v, right_v, right_prod_v)
    copies = [
        pltpu.make_async_copy(source, target, load_sem.at[i])
        for i, (source, target) in enumerate(zip(sources, targets))
    ]
    for copy in copies:
        copy.start()
    copies[0].wait()
    for j in range(col_blocks):
        update[:, :, j, :] = tiles_v[:, :, j * share : (j + 1) * share]
    copies[1].wait()
    copies[2].wait()
    left_out[...] = decay_rate * left_v[...] + (1.0 - decay_rate) * left_prod_v[...]
    copies[3].wait()
    copies[4].wait()
    right_out[...] = decay_rate * right_v[...] + (1.0 - decay_rate) * right_prod_v[...]


def on_device(acts, dout, left_stats, right_stats, left_root, right_root, owner_of, counters):
    replicas, owners = lax.axis_size("dp"), lax.axis_size("owner")
    tokens, features = acts.shape
    col_blocks, share = dout.shape[1:]
    slots, rows, order = left_stats.shape
    row_blocks = features // order
    chips = replicas // 2
    half = chips // 2
    f32, bf16 = jnp.float32, jnp.bfloat16
    total = counters.shape[0]
    dout_rows = dout.transpose(1, 2, 0).reshape(col_blocks * share, tokens)
    vmem = functools.partial(pl.BlockSpec, memory_space=pltpu.VMEM)
    anywhere = functools.partial(pl.BlockSpec, memory_space=pl.ANY)
    kept = slots // 2
    ring_shape = (2, RING_GROUPS, half + 1, row_blocks // RING_GROUPS, rows, LANES)
    dma = pltpu.SemaphoreType.DMA
    left_prod, right_prod, update = pl.pallas_call(
        step_kernel,
        out_shape=(
            jax.ShapeDtypeStruct((slots, rows, order), f32),
            jax.ShapeDtypeStruct((slots, rows, order), f32),
            jax.ShapeDtypeStruct((row_blocks, rows, LANES), bf16),
        ),
        in_specs=[anywhere()] * 6,
        out_specs=(vmem(), vmem(), vmem()),
        scratch_shapes=[
            pltpu.VMEM((1, total), jnp.int32),
            pltpu.VMEM((1, total), jnp.int32),
            pltpu.VMEM((8, LANES), jnp.int32),
            pltpu.SMEM((8, LANES), jnp.int32),
            pltpu.VMEM((row_blocks, tokens, order), bf16),
            pltpu.VMEM((LANES, tokens), bf16),
            pltpu.VMEM((slots, rows, order), bf16),
            pltpu.VMEM((2, kept, rows, order), bf16),
            pltpu.VMEM((kept, order, order), bf16),
            pltpu.VMEM((row_blocks, chips, 2, rows, LANES), bf16),
            pltpu.VMEM((row_blocks, chips, rows, LANES), bf16),
            pltpu.VMEM(ring_shape, bf16),
            pltpu.VMEM(ring_shape, bf16),
            pltpu.VMEM((row_blocks * col_blocks + 1, rows, LANES), f32),
            pltpu.VMEM((owners, rows, LANES), bf16),
            pltpu.VMEM((owners, rows, LANES), bf16),
            pltpu.VMEM((slots, rows, order), bf16),
            pltpu.VMEM((replicas, kept, rows, order), bf16),
            pltpu.VMEM((kept, LANES // (2 * rows), 2 * rows, order), bf16),
            pltpu.VMEM((2, kept, rows, order), bf16),
            pltpu.VMEM((slots, rows, order), bf16),
            pltpu.VMEM((2, 2, kept, rows, order), f32),
            pltpu.VMEM((2, kept, rows, order), f32),
            pltpu.VMEM((1, LANES), f32),
            pltpu.VMEM((replicas, 1, LANES), f32),
            pltpu.VMEM((owners, rows, LANES), f32),
            pltpu.VMEM((owners, rows, LANES), f32),
            pltpu.VMEM((owners, rows, LANES), bf16),
            pltpu.VMEM((owners, rows, LANES), bf16),
            pltpu.VMEM((owners * col_blocks, rows, LANES), f32),
            dma((row_blocks,)),
            dma((6,)),
            dma((row_blocks,)),
            dma((row_blocks,)),
            dma((2, RING_GROUPS, half + 1)),
            dma((2, RING_GROUPS, half + 1)),
            dma,
            dma,
            dma((2, half)),
            dma((2, half)),
            dma((4,)),
            dma((4,)),
            dma,
            dma,
            dma,
            dma,
        ],
        compiler_params=pltpu.CompilerParams(
            collective_id=0, has_side_effects=True, vmem_limit_bytes=56 * 1024 * 1024
        ),
    )(owner_of.reshape(1, total), counters.reshape(1, total), dout_rows, acts, left_root, right_root)
    return pl.pallas_call(
        finish_kernel,
        out_shape=(
            jax.ShapeDtypeStruct((slots, rows, order), f32),
            jax.ShapeDtypeStruct((slots, rows, order), f32),
            jax.ShapeDtypeStruct((row_blocks, rows, col_blocks, share), bf16),
        ),
        in_specs=[anywhere()] * 5,
        out_specs=(vmem(), vmem(), vmem()),
        scratch_shapes=[pltpu.VMEM((slots, rows, order), f32)] * 4
        + [pltpu.VMEM((row_blocks, rows, LANES), bf16), dma((5,))],
    )(left_stats, right_stats, left_prod, right_prod, update)


def solution(mesh):
    in_specs = (
        P("dp", None),
        P("dp", None, "owner"),
        P("owner", "dp", None),
        P("owner", "dp", None),
        P("owner", "dp", None),
        P("owner", None, None),
        P(),
        P(),
    )
    out_specs = (P("owner", "dp", None), P("owner", "dp", None), P(None, "dp", None, "owner"))
    return jax.shard_map(
        on_device, mesh=mesh, in_specs=in_specs, out_specs=out_specs, check_vma=False
    )
```

```python
import functools

import jax
import jax.numpy as jnp
from jax import lax
from jax.experimental import pallas as pl
from jax.experimental.pallas import tpu as pltpu
from jax.sharding import PartitionSpec as P

WARMUP = 25
MESH = pl.DeviceIdType.MESH
LANES = 128
RING_GROUPS = 2
STOP = {1: 0, 2: 0, 3: 2, 4: 2, 5: 0, 6: 5, 7: 5, 8: 5}

decay_rate = 0.95
epsilon = 1e-06


def around(place, size):
    place = jnp.where(place >= size, place - size, place)
    return jnp.where(place < 0, place + size, place)


def far_first(size):
    return [(size // 2 + ((k + 1) // 2 if k % 2 else -(k // 2))) % size for k in range(size)]


def swing(size, visit):
    def step(k, carry):
        distance, stride, side = carry
        visit(distance)
        return distance + side * stride, stride + 1, -side

    lax.fori_loop(0, size - 1, step, (jnp.int32(size // 2), jnp.int32(1), jnp.int32(1)))


def place_tables(owner_row, counter_row, slot_count, col_blocks):
    total = owner_row.shape[1]
    square = (total, total)
    down = lax.broadcasted_iota(jnp.int32, square, 0)
    across = lax.broadcasted_iota(jnp.int32, square, 1)

    def upright(row):
        return jnp.sum(jnp.where(down == across, row, 0), axis=1, keepdims=True)

    owner_col, counter_col = upright(owner_row), upright(counter_row)
    same = owner_col == owner_row
    slot_col = jnp.sum(jnp.where(same & (across < down), 1, 0), axis=1, keepdims=True)
    slot_row = jnp.sum(jnp.where(same & (down < across), 1, 0), axis=0, keepdims=True)
    block_col, block_row = down[:, :1], across[:1, :]
    last = col_blocks - 1
    taken = (block_col & ~last) + ((slot_col - block_col) & last)
    given = owner_row * col_blocks + ((block_row - slot_row) & last)
    places = lax.broadcasted_iota(jnp.int32, (total, LANES), 1)
    hit = owner_col * slot_count + slot_col == places
    source = total + jnp.sum(jnp.where(hit, taken - total, 0), axis=0, keepdims=True)
    begun = jnp.sum(jnp.where(hit & (counter_col >= WARMUP), 1, 0), axis=0, keepdims=True)
    return source, given, begun


def step_kernel(
    owner_hbm,
    counter_hbm,
    dout_hbm,
    acts_hbm,
    left_root_hbm,
    right_root_hbm,
    left_prod,
    right_prod,
    update,
    owner_v,
    counter_v,
    table_v,
    table,
    acts_v,
    dout_v,
    left_root,
    roots,
    right_root,
    terms,
    sibling_terms,
    sum_out,
    sum_in,
    turned,
    tile_out,
    tile_in,
    own_grad,
    grads,
    flipped,
    pre_out,
    precond,
    prod_out,
    prod_in,
    norm_out,
    norm_in,
    pre_tiles,
    grad_tiles,
    result_out,
    result_in,
    returned,
    acts_sem,
    load_sem,
    pair_send,
    pair_recv,
    ring_send,
    ring_recv,
    tile_send,
    tile_recv,
    gather_send,
    gather_recv,
    swap_send,
    swap_recv,
    norm_send,
    norm_recv,
    result_send,
    result_recv,
):
    replica = lax.axis_index("dp")
    owner = lax.axis_index("owner")
    replicas = grads.shape[0]
    owners = tile_in.shape[0]
    chips = replicas // 2
    half = chips // 2
    chip = replica // 2
    core = lax.rem(replica, 2)
    row_blocks, tokens, order = acts_v.shape
    slots, rows, _ = own_grad.shape
    col_blocks = turned.shape[0] // row_blocks
    share = LANES // col_blocks
    group_rows = row_blocks // RING_GROUPS
    kept = slots // 2
    mine = pl.ds(core * kept, kept)
    theirs = pl.ds((1 - core) * kept, kept)
    f32, bf16 = jnp.float32, jnp.bfloat16

    def acts_copy(i):
        return pltpu.make_async_copy(
            acts_hbm.at[:, pl.ds(pl.multiple_of(i * order, order), order)],
            acts_v.at[i],
            acts_sem.at[i],
        )

    dout_copy = pltpu.make_async_copy(dout_hbm, dout_v, load_sem.at[0])
    left_copy = pltpu.make_async_copy(left_root_hbm, left_root, load_sem.at[1])
    right_copy = pltpu.make_async_copy(right_root_hbm.at[mine], right_root, load_sem.at[2])
    owner_copy = pltpu.make_async_copy(owner_hbm, owner_v, load_sem.at[3])
    counter_copy = pltpu.make_async_copy(counter_hbm, counter_v, load_sem.at[4])
    table_copy = pltpu.make_async_copy(table_v, table, load_sem.at[5])
    owner_copy.start()
    counter_copy.start()
    dout_copy.start()
    for i in range(row_blocks):
        acts_copy(i).start()
    left_copy.start()
    right_copy.start()

    across = min(4, owners)

    high, wide = owner // across, lax.rem(owner, across)
    beside = [around(wide + d, across) for d in far_first(across)]

    def each_owner(visit):
        def row(distance):
            y = around(high + distance, owners // across) * across
            visit([y + x for x in beside])

        swing(owners // across, row)
        visit([high * across + x for x in beside[:-1]])

    def each_replica(visit):
        def both(distance):
            there = around(chip + distance, chips) * 2
            visit(there)
            visit(there + 1)

        swing(chips, both)
        visit(chip * 2 + 1 - core)

    barrier = pltpu.get_barrier_semaphore()

    def greet_owner(peers):
        for peer in peers:
            pl.semaphore_signal(barrier, inc=1, device_id=(replica, peer), device_id_type=MESH)

    def greet_replica(peer):
        pl.semaphore_signal(barrier, inc=1, device_id=(peer, owner), device_id_type=MESH)

    each_replica(greet_replica)
    each_owner(greet_owner)
    turned[row_blocks * col_blocks] = jnp.zeros((rows, LANES), f32)
    owner_copy.wait()
    counter_copy.wait()
    source, given, begun = place_tables(owner_v[...], counter_v[...], slots, col_blocks)
    table_v[0:1, :] = source
    table_v[1:2, 0 : row_blocks * col_blocks] = given
    table_v[2:3, :] = begun
    table_copy.start()
    dout_copy.wait()

    sibling = (chip * 2 + 1 - core, owner)
    up = (around(chip + 1, chips) * 2 + core, owner)
    down = (around(chip - 1, chips) * 2 + core, owner)

    def pair_copy(i):
        return pltpu.make_async_remote_copy(
            src_ref=terms.at[i, :, 1 - core],
            dst_ref=sibling_terms.at[i],
            send_sem=pair_send.at[i],
            recv_sem=pair_recv.at[i],
            device_id=sibling,
            device_id_type=MESH,
        )

    def term_step(i, carry):
        acts_copy(i).wait()
        part = jnp.dot(dout_v[...], acts_v[i], preferred_element_type=f32)
        terms[i] = part.T.astype(bf16).reshape(chips, 2, rows, LANES)
        return carry

    def term_and_pair(i, carry):
        term_step(i, carry)
        pair_copy(i).start()
        return carry

    early = row_blocks * 3 // 4
    lax.fori_loop(0, early, term_step, 0)
    pl.semaphore_wait(barrier, owners + replicas - 2)
    for i in range(early):
        pair_copy(i).start()
    lax.fori_loop(early, row_blocks, term_and_pair, 0)

    def swap_copy(which, source, target):
        return pltpu.make_async_remote_copy(
            src_ref=source,
            dst_ref=target,
            send_sem=swap_send.at[which],
            recv_sem=swap_recv.at[which],
            device_id=sibling,
            device_id_type=MESH,
        )

    root_swap = swap_copy(0, left_root.at[theirs], roots.at[core])
    grad_swap = swap_copy(1, own_grad.at[theirs], grads.at[replica])
    pre_swap = swap_copy(2, pre_out.at[1 - core], precond.at[mine])
    prod_swap = swap_copy(3, prod_out.at[1 - core], prod_in)
    left_copy.wait()
    root_swap.start()
    roots[core] = left_root[mine]

    def sum_copy(way, group, hops):
        step = hops - STOP[hops]
        peer = around(chip + (-step if way else step), chips) * 2 + core
        return pltpu.make_async_remote_copy(
            src_ref=sum_out.at[way, group, hops],
            dst_ref=sum_in.at[way, group, hops],
            send_sem=ring_send.at[way, group, hops],
            recv_sem=ring_recv.at[way, group, hops],
            device_id=(peer, owner),
            device_id_type=MESH,
        )

    def chip_terms(group, piece):
        here = pl.ds(group * group_rows, group_rows)
        return terms[here, piece, core].astype(f32) + sibling_terms[here, piece].astype(f32)

    def arrived(way, group, hops):
        sum_copy(way, group, hops).wait_recv()
        return sum_in[way, group, hops].astype(f32)

    def pass_on(way, group, hops):
        total = chip_terms(group, around(chip + (-hops if way else hops), chips))
        for other in routes[way]:
            if STOP[other] == hops:
                total = total + arrived(way, group, other)
        sum_out[way, group, hops] = total.astype(bf16)
        sum_copy(way, group, hops).start()

    routes = [range(1, half + 1), range(1, half)]
    for group in range(RING_GROUPS):
        for i in range(group * group_rows, (group + 1) * group_rows):
            pair_copy(i).wait_recv()
        for hops in range(half, 0, -1):
            for way in range(2):
                if hops in routes[way] and STOP[hops]:
                    pass_on(way, group, hops)
    for group in range(RING_GROUPS):
        for hops in range(half, 0, -1):
            for way in range(2):
                if hops in routes[way] and not STOP[hops]:
                    pass_on(way, group, hops)

    for group in range(RING_GROUPS):
        total = chip_terms(group, chip)
        for hops in range(1, half + 1):
            for way in range(2):
                if hops in routes[way] and not STOP[hops]:
                    total = total + arrived(way, group, hops)
        total = total.astype(bf16).astype(f32)
        for i in range(group_rows):
            for k in range(col_blocks):
                tile = total[i] if k == 0 else pltpu.roll(total[i], k * share, 1)
                turned[(group * group_rows + i) * col_blocks + k] = tile

    lane_block = lax.broadcasted_iota(jnp.int32, (rows, LANES), 1) // share

    table_copy.wait()

    def tile_copy(peer):
        return pltpu.make_async_remote_copy(
            src_ref=tile_out.at[peer],
            dst_ref=tile_in.at[owner],
            send_sem=tile_send,
            recv_sem=tile_recv,
            device_id=(replica, peer),
            device_id_type=MESH,
        )

    def tiles_for(peer):
        tile = jnp.zeros((rows, LANES), f32)
        for s in range(slots):
            tile = jnp.where(lane_block == s, turned[table[0, peer * slots + s]], tile)
        return tile.astype(bf16)

    def tile_step(peers):
        tiles = [tiles_for(peer) for peer in peers]
        for peer, tile in zip(peers, tiles):
            tile_out[peer] = tile
        for peer in peers:
            tile_copy(peer).start()

    each_owner(tile_step)
    tile_in[owner] = tiles_for(owner)
    others = pl.ds(0, owners - 1)
    pltpu.make_async_copy(tile_in.at[others], tile_in.at[others], tile_recv).wait()

    pieces = [tile_in[o].astype(f32) for o in range(owners)]
    for s in range(slots):
        for q in range(order // LANES):
            tile = jnp.zeros((rows, LANES), f32)
            for k in range(col_blocks):
                shift = (k - s) * share % LANES
                piece = pieces[q * col_blocks + k]
                piece = pltpu.roll(piece, shift, 1) if shift else piece
                tile = jnp.where(lane_block == k, piece, tile)
            own_grad[s, :, q * LANES : (q + 1) * LANES] = tile.astype(bf16)
    grad_swap.start()
    grads[replica] = own_grad[mine]

    def gather_copy(way, step):
        there = around(chip + (step if way else -step), chips)
        piece = grads.at[pl.ds(there * 2, 2)]
        return pltpu.make_async_remote_copy(
            src_ref=piece,
            dst_ref=piece,
            send_sem=gather_send.at[way, step],
            recv_sem=gather_recv.at[way, step],
            device_id=down if way else up,
            device_id_type=MESH,
        )

    grad_swap.wait_recv()
    gather_copy(0, 0).start()
    if half > 1:
        gather_copy(1, 0).start()

    lane = lax.broadcasted_iota(jnp.int32, (1, LANES), 1)
    norms = jnp.zeros((1, LANES), f32)
    for s in range(slots):
        own = own_grad[s].astype(f32)
        square = jnp.sum(own * own, axis=(0, 1), keepdims=True)
        norms = jnp.where(lane == slots + s, square, norms)

    def gather_round(step, carry):
        for way in range(2):
            gather_copy(way, step - 1).wait_recv()
            gather_copy(way, step).start()
        return carry

    lax.fori_loop(1, half - 1, gather_round, 0)
    if half > 1:
        gather_copy(0, half - 2).wait_recv()
        gather_copy(0, half - 1).start()
    root_swap.wait_recv()
    right_copy.wait()
    if half > 1:
        gather_copy(1, half - 2).wait_recv()
    gather_copy(0, half - 1).wait_recv()

    for t in range(kept):
        whole = grads[:, t].reshape(order, order)
        root = roots[:, t].reshape(2 * rows, order)
        inner = jnp.dot(root, whole, preferred_element_type=f32).astype(bf16)
        pre = jnp.dot(inner, right_root[t], preferred_element_type=f32).astype(bf16)
        pre_out[:, t] = pre.reshape(2, rows, order)
        pre = pre.astype(f32)
        square = jnp.sum(pre * pre, axis=(0, 1), keepdims=True)
        norms = jnp.where(lane == core * kept + t, square, norms)
    norm_out[...] = norms

    def norm_copy(peer):
        return pltpu.make_async_remote_copy(
            src_ref=norm_out,
            dst_ref=norm_in.at[replica],
            send_sem=norm_send,
            recv_sem=norm_recv,
            device_id=(peer, owner),
            device_id_type=MESH,
        )

    def norm_step(peer):
        norm_copy(peer).start()

    each_replica(norm_step)
    pre_swap.start()
    norm_in[replica] = norms
    precond[mine] = pre_out[core]

    span = pl.ds(pl.multiple_of(chip * 2 * rows // LANES * LANES, LANES), LANES)
    for t in range(kept):
        whole = grads[:, t].reshape(order, order)
        both = grads[pl.ds(chip * 2, 2), t].reshape(2 * rows, order)
        left = lax.dot_general(
            both, whole, (((1,), (1,)), ((), ())), preferred_element_type=f32
        )
        columns = grads[:, t, :, span].reshape(order, LANES)
        flipped[t] = columns.T.reshape(LANES // (2 * rows), 2 * rows, order)
        turned_rows = flipped[t, lax.rem(chip, LANES // (2 * rows))]
        right = jnp.dot(turned_rows, whole, preferred_element_type=f32)
        prod_out[:, 0, t] = left.reshape(2, rows, order)
        prod_out[:, 1, t] = right.reshape(2, rows, order)
    prod_swap.start()
    left_prod[mine] = prod_out[core, 0]
    right_prod[mine] = prod_out[core, 1]

    pre_swap.wait_recv()

    for q in range(order // LANES):
        here = slice(q * LANES, (q + 1) * LANES)
        pre_parts = [precond[s, :, here].astype(f32) for s in range(slots)]
        own_parts = [own_grad[s, :, here].astype(f32) for s in range(slots)]
        for k in range(col_blocks):
            pre_tile = jnp.zeros((rows, LANES), f32)
            own_tile = jnp.zeros((rows, LANES), f32)
            for s in range(slots):
                shift = (s - k) * share % LANES
                pre_part, own_part = pre_parts[s], own_parts[s]
                if shift:
                    pre_part = pltpu.roll(pre_part, shift, 1)
                    own_part = pltpu.roll(own_part, shift, 1)
                pre_tile = jnp.where(lane_block == s, pre_part, pre_tile)
                own_tile = jnp.where(lane_block == s, own_part, own_tile)
            pre_tiles[q * col_blocks + k] = pre_tile
            grad_tiles[q * col_blocks + k] = own_tile

    other_replicas = pl.ds(0, replicas - 1)
    pltpu.make_async_copy(
        norm_in.at[other_replicas], norm_in.at[other_replicas], norm_recv
    ).wait()
    norms = jnp.sum(norm_in[...], axis=0)
    scale = jnp.zeros((1, LANES), f32)
    started = jnp.zeros((1, LANES), jnp.int32)
    for s in range(slots):
        graft = jnp.sqrt(norms[:, slots + s : slots + s + 1] / (norms[:, s : s + 1] + epsilon))
        scale = jnp.where(lane // share == s, graft, scale)
        started = jnp.where(lane // share == s, table[2, owner * slots + s], started)

    def result_copy(peer):
        return pltpu.make_async_remote_copy(
            src_ref=result_out.at[peer],
            dst_ref=result_in.at[owner],
            send_sem=result_send,
            recv_sem=result_recv,
            device_id=(replica, peer),
            device_id_type=MESH,
        )

    def result_for(peer):
        return jnp.where(started > 0, pre_tiles[peer] * scale, grad_tiles[peer]).astype(bf16)

    def result_step(peers):
        results = [result_for(peer) for peer in peers]
        for peer, result in zip(peers, results):
            result_out[peer] = result
        for peer in peers:
            result_copy(peer).start()

    each_owner(result_step)
    result_in[owner] = result_for(owner)

    pltpu.make_async_copy(result_in.at[others], result_in.at[others], result_recv).wait()

    batch = min(8, owners)

    def turn_step(n, carry):
        for o in range(batch):
            tile = result_in[n * batch + o].astype(f32)
            for k in range(col_blocks):
                place = (n * batch + o) * col_blocks + k
                returned[place] = pltpu.roll(tile, k * share, 1) if k else tile
        return carry

    lax.fori_loop(0, owners // batch, turn_step, 0)

    for i in range(row_blocks):
        tile = jnp.zeros((rows, LANES), f32)
        for j in range(col_blocks):
            tile = jnp.where(lane_block == j, returned[table[1, i * col_blocks + j]], tile)
        update[i] = tile.astype(bf16)

    prod_swap.wait_recv()
    left_prod[theirs] = prod_in[0]
    right_prod[theirs] = prod_in[1]

    root_swap.wait_send()
    grad_swap.wait_send()
    pre_swap.wait_send()
    prod_swap.wait_send()
    for i in range(row_blocks):
        pair_copy(i).wait_send()

    def sent(step, carry):
        for way in range(2):
            gather_copy(way, step).wait_send()
        return carry

    lax.fori_loop(0, half - 1, sent, 0)
    for way in range(2):
        for group in range(RING_GROUPS):
            for hops in routes[way]:
                sum_copy(way, group, hops).wait_send()
    gather_copy(0, half - 1).wait_send()
    pltpu.make_async_copy(tile_in.at[others], tile_in.at[others], tile_send).wait()
    pltpu.make_async_copy(
        norm_in.at[other_replicas], norm_in.at[other_replicas], norm_send
    ).wait()
    pltpu.make_async_copy(result_in.at[others], result_in.at[others], result_send).wait()


def finish_kernel(
    left_stats,
    right_stats,
    left_prod,
    right_prod,
    tiles,
    left_out,
    right_out,
    update,
    left_v,
    right_v,
    left_prod_v,
    right_prod_v,
    tiles_v,
    load_sem,
):
    col_blocks, share = update.shape[2:]
    sources = (tiles, left_stats, left_prod, right_stats, right_prod)
    targets = (tiles_v, left_v, left_prod_v, right_v, right_prod_v)
    copies = [
        pltpu.make_async_copy(source, target, load_sem.at[i])
        for i, (source, target) in enumerate(zip(sources, targets))
    ]
    for copy in copies:
        copy.start()
    copies[0].wait()
    for j in range(col_blocks):
        update[:, :, j, :] = tiles_v[:, :, j * share : (j + 1) * share]
    copies[1].wait()
    copies[2].wait()
    left_out[...] = decay_rate * left_v[...] + (1.0 - decay_rate) * left_prod_v[...]
    copies[3].wait()
    copies[4].wait()
    right_out[...] = decay_rate * right_v[...] + (1.0 - decay_rate) * right_prod_v[...]


def on_device(acts, dout, left_stats, right_stats, left_root, right_root, owner_of, counters):
    replicas, owners = lax.axis_size("dp"), lax.axis_size("owner")
    tokens, features = acts.shape
    col_blocks, share = dout.shape[1:]
    slots, rows, order = left_stats.shape
    row_blocks = features // order
    chips = replicas // 2
    half = chips // 2
    f32, bf16 = jnp.float32, jnp.bfloat16
    total = counters.shape[0]
    dout_rows = dout.transpose(1, 2, 0).reshape(col_blocks * share, tokens)
    vmem = functools.partial(pl.BlockSpec, memory_space=pltpu.VMEM)
    anywhere = functools.partial(pl.BlockSpec, memory_space=pl.ANY)
    kept = slots // 2
    ring_shape = (2, RING_GROUPS, half + 1, row_blocks // RING_GROUPS, rows, LANES)
    dma = pltpu.SemaphoreType.DMA
    left_prod, right_prod, update = pl.pallas_call(
        step_kernel,
        out_shape=(
            jax.ShapeDtypeStruct((slots, rows, order), f32),
            jax.ShapeDtypeStruct((slots, rows, order), f32),
            jax.ShapeDtypeStruct((row_blocks, rows, LANES), bf16),
        ),
        in_specs=[anywhere()] * 6,
        out_specs=(vmem(), vmem(), vmem()),
        scratch_shapes=[
            pltpu.VMEM((1, total), jnp.int32),
            pltpu.VMEM((1, total), jnp.int32),
            pltpu.VMEM((8, LANES), jnp.int32),
            pltpu.SMEM((8, LANES), jnp.int32),
            pltpu.VMEM((row_blocks, tokens, order), bf16),
            pltpu.VMEM((LANES, tokens), bf16),
            pltpu.VMEM((slots, rows, order), bf16),
            pltpu.VMEM((2, kept, rows, order), bf16),
            pltpu.VMEM((kept, order, order), bf16),
            pltpu.VMEM((row_blocks, chips, 2, rows, LANES), bf16),
            pltpu.VMEM((row_blocks, chips, rows, LANES), bf16),
            pltpu.VMEM(ring_shape, bf16),
            pltpu.VMEM(ring_shape, bf16),
            pltpu.VMEM((row_blocks * col_blocks + 1, rows, LANES), f32),
            pltpu.VMEM((owners, rows, LANES), bf16),
            pltpu.VMEM((owners, rows, LANES), bf16),
            pltpu.VMEM((slots, rows, order), bf16),
            pltpu.VMEM((replicas, kept, rows, order), bf16),
            pltpu.VMEM((kept, LANES // (2 * rows), 2 * rows, order), bf16),
            pltpu.VMEM((2, kept, rows, order), bf16),
            pltpu.VMEM((slots, rows, order), bf16),
            pltpu.VMEM((2, 2, kept, rows, order), f32),
            pltpu.VMEM((2, kept, rows, order), f32),
            pltpu.VMEM((1, LANES), f32),
            pltpu.VMEM((replicas, 1, LANES), f32),
            pltpu.VMEM((owners, rows, LANES), f32),
            pltpu.VMEM((owners, rows, LANES), f32),
            pltpu.VMEM((owners, rows, LANES), bf16),
            pltpu.VMEM((owners, rows, LANES), bf16),
            pltpu.VMEM((owners * col_blocks, rows, LANES), f32),
            dma((row_blocks,)),
            dma((6,)),
            dma((row_blocks,)),
            dma((row_blocks,)),
            dma((2, RING_GROUPS, half + 1)),
            dma((2, RING_GROUPS, half + 1)),
            dma,
            dma,
            dma((2, half)),
            dma((2, half)),
            dma((4,)),
            dma((4,)),
            dma,
            dma,
            dma,
            dma,
        ],
        compiler_params=pltpu.CompilerParams(
            collective_id=0, has_side_effects=True, vmem_limit_bytes=56 * 1024 * 1024
        ),
    )(owner_of.reshape(1, total), counters.reshape(1, total), dout_rows, acts, left_root, right_root)
    return pl.pallas_call(
        finish_kernel,
        out_shape=(
            jax.ShapeDtypeStruct((slots, rows, order), f32),
            jax.ShapeDtypeStruct((slots, rows, order), f32),
            jax.ShapeDtypeStruct((row_blocks, rows, col_blocks, share), bf16),
        ),
        in_specs=[anywhere()] * 5,
        out_specs=(vmem(), vmem(), vmem()),
        scratch_shapes=[pltpu.VMEM((slots, rows, order), f32)] * 4
        + [pltpu.VMEM((row_blocks, rows, LANES), bf16), dma((5,))],
    )(left_stats, right_stats, left_prod, right_prod, update)


def solution(mesh):
    in_specs = (
        P("dp", None),
        P("dp", None, "owner"),
        P("owner", "dp", None),
        P("owner", "dp", None),
        P("owner", "dp", None),
        P("owner", None, None),
        P(),
        P(),
    )
    out_specs = (P("owner", "dp", None), P("owner", "dp", None), P(None, "dp", None, "owner"))
    return jax.shard_map(
        on_device, mesh=mesh, in_specs=in_specs, out_specs=out_specs, check_vma=False
    )
```
